256 devices in a mesh: width: 16 (over y, x_hi, core), feat: 16 (over x_lo, z).
Axes of the slice: x: 4 (x_hi: 2, x_lo: 2; x = x_hi * 2 + x_lo), y: 4, z: 8, core: 2. Of those that a mesh axis runs over, the one named last changes fastest.
Arguments:
- acts: bfloat16 [4096, 2, 8192], P('feat', None, 'width'), may hold values from -6 to 6
- enc_weight: bfloat16 [16, 2, 8192, 1024], P('feat', None, 'width'), may hold values from -0.046875 to 0.046875
- enc_bias: float32 [16, 1024], P('feat'), may hold values from -6 to 6
- dec_weight: bfloat16 [16, 1024, 2, 8192], P('feat', None, None, 'width'), may hold values from -1 to 1
- dec_bias: float32 [2, 8192], P(None, 'width'), may hold values from -4 to 4
- routes: int32 [4096, 2], P('feat'), may hold values from 0 to 15, all different within a row; in each aligned block of 256 rows (0 to 255, 256 to 511, ...) at most 64 rows name the same one
- latent_index: int32 [4096, 2, 32], P('feat'), may hold values from 0 to 1023, as said below
Outputs:
- grad_enc: bfloat16 [16, 2, 8192, 1024], P('feat', None, 'width')
- grad_dec: bfloat16 [16, 1024, 2, 8192], P('feat', None, None, 'width')
The draws below stay inside these ranges and needn't reach their ends.
Inputs may be any that keep to these rules, and one draw needn't show every extreme that they name: `routes`: within the 256 rows of one device no expert is named by more than 64 rows, a bound that some block reaches. `latent_index`: the 32 latents of one token and route are distinct.
All inputs are finite; a program needn't handle non-finite values.
Results may differ from the reference program's by a relative error of at most 0.0057.
Values may be sent and summed in bfloat16 or wider, within the bound.
No kernel may reach another device: no remote copies, remote signals or barrier semaphores. Data moves between devices by JAX's collectives and lax.ppermute only.
A program may use at most 128 MiB of HBM per device.

```python
import math
import jax
import jax.numpy as jnp
import numpy as np
from jax import lax

D = 8192
F = 1024
L = 2
TOP = 2
K = 32
TOK_DEV = 256
EXPERTS = 16
TOKENS = 4096
CAP = 64
N_FEAT = 16


def draw_latent_index(key, part):
    key = jax.random.fold_in(key, 7)
    row_total = TOKENS * TOP
    scores = jax.random.randint(key, (row_total, F), 0, 1048576, dtype=jnp.int32)
    scores = scores * F + jnp.arange(F, dtype=jnp.int32)[None, :]
    chosen = lax.top_k(scores, K)[1]
    return chosen.astype(jnp.int32).reshape(TOKENS, TOP, K)


def level_of(rng, dims, split, low, largest):
    def one(dim, blocks):
        steps = jax.random.uniform(jax.random.fold_in(jax.random.fold_in(rng, 6), dim), (blocks,), jnp.float32, low / len(split), largest / len(split))
        return jnp.repeat(jnp.exp(steps), dims[dim] // blocks).reshape((-1,) + (1,) * (len(dims) - dim - 1))

    factor_of = one(*split[0])
    for cut in split[1:]:
        factor_of = factor_of * one(*cut)
    return factor_of


def assign_block(rng, own, number, rows, count, top, reach, skew):
    ranking = jax.random.permutation(rng, count)
    crowded, common = portions_of(count, rows * top, reach, skew, True), portions_of(count, rows * top, reach, skew, False)
    places = jnp.arange(count)

    def named(tallies, rotation):
        used = int((tallies > 0).sum())
        fixed = max(1, used // 4)
        moved = fixed + (places - fixed + rotation * (used - fixed)) % max(1, count - fixed)
        return jnp.zeros((count,), jnp.int32).at[ranking[jnp.where(places < fixed, places, moved)]].set(jnp.asarray(tallies, jnp.int32))

    tallies = jnp.where(number % 4 == 0, named(crowded, number // 4), named(common, number - number // 4 - 1))
    mixed = jax.random.permutation(jax.random.fold_in(own, 3), count)
    giver, taker = mixed[0:count // 2 * 2:2], mixed[1:count // 2 * 2:2]
    margin = jnp.minimum(tallies[giver] - 1, reach - tallies[taker]) // 2
    margin = jnp.where((giver == ranking[0]) | (taker == ranking[0]) | (tallies[taker] == 0), 0, jnp.maximum(margin, 0))
    moved = jax.random.randint(jax.random.fold_in(own, 4), (count // 2,), 0, 1 << 20) % (margin + 1)
    tallies = tallies.at[giver].add(-moved).at[taker].add(moved)
    items = jnp.searchsorted(jnp.cumsum(tallies), jnp.arange(rows * top), side="right").astype(jnp.int32)
    table = items.reshape(top, rows).T
    table = table[jax.random.permutation(jax.random.fold_in(own, 1), rows)]
    rotation = jax.random.randint(jax.random.fold_in(own, 2), (rows, 1), 0, top)
    return jnp.take_along_axis(table, (jnp.arange(top)[None, :] + rotation) % top, axis=1)


def portions_of(count, total, limit, lean, full):
    loads = [(1 << 20) // math.isqrt(rank ** lean) + 1 for rank in range(1, count + 1)]
    largest = limit if full else min(limit, max(-(-total // count), total * loads[0] // sum(loads)))
    least = 1 if total - largest >= count - 1 else 0
    holding, spare = [largest] + [least] * (count - 1), total - largest - least * (count - 1)
    while spare > 0:
        candidates = [i for i in range(1, count) if holding[i] < largest] or [i for i in range(1, count) if holding[i] < limit]
        pool, budget = sum([loads[i] for i in candidates]), spare
        for i in candidates:
            more = min(limit - holding[i], max(1, budget * loads[i] // pool), spare)
            holding[i] = holding[i] + more
            spare = spare - more
    return np.array(holding)


def gaussian(rng, extent, scale, most, split=(), kind=jnp.bfloat16):
    result = jax.random.normal(rng, extent, jnp.float32) * scale
    if len(split) > 0:
        result = level_of(rng, extent, split, -0.22, 0.18) * result
    return jnp.clip(result, min=-most, max=most).astype(kind)


def setup_inputs(seed: int = 0) -> dict:
    keys = jax.random.split(jax.random.key(seed), 8)
    acts = gaussian(keys[0], (TOKENS, L, D), 1.0, 6.0, ((0, 16), (2, 16)))
    enc_weight = gaussian(keys[1], (EXPERTS, L, D, F), (L * D) ** -0.5, 0.046875, ((0, 16), (2, 16)))
    enc_bias = gaussian(keys[2], (EXPERTS, F), 1.0, 6.0, ((0, 16),), jnp.float32)
    dec_weight = gaussian(keys[3], (EXPERTS, F, L, D), K ** -0.5, 1.0, ((0, 16), (3, 16)))
    dec_bias = gaussian(keys[4], (L, D), 0.5, 4.0, ((1, 16),), jnp.float32)
    routes_keys = jax.random.split(jax.random.fold_in(keys[5], 1), TOKENS // TOK_DEV)
    routes_turns = jax.random.permutation(jax.random.fold_in(keys[5], 3), TOKENS // TOK_DEV)
    routes = jax.vmap(lambda own, number: assign_block(jax.random.fold_in(keys[5], 2), own, number, TOK_DEV, EXPERTS, TOP, CAP, 2))(routes_keys, routes_turns).reshape((TOKENS, TOP))
    latent_index = draw_latent_index(jax.random.fold_in(keys[7], 71), 0)
    return dict(acts=acts, enc_weight=enc_weight, enc_bias=enc_bias, dec_weight=dec_weight, dec_bias=dec_bias, routes=routes, latent_index=latent_index)


def silu_grad(value):
    sigmoid_value = jax.nn.sigmoid(value)
    return sigmoid_value * (1.0 + value * (1.0 - sigmoid_value))

def latent_mask(index_rows, latents):
    row_ids = jnp.arange(index_rows.shape[0], dtype=jnp.int32)[:, None]
    empty_mask = jnp.zeros((index_rows.shape[0], latents), jnp.bool_)
    return empty_mask.at[row_ids, index_rows].set(True, mode='drop')

def reference(acts, enc_weight, enc_bias, dec_weight, dec_bias, routes, latent_index):
    inner_width = L * D
    row_total = TOKENS * TOP
    slot_count = N_FEAT * CAP
    scale_factor = 1.0 / math.sqrt(L * D)
    flat_acts = acts.reshape(TOKENS, inner_width)
    flat_routes = routes.reshape(row_total)
    flat_index = latent_index.reshape(row_total, K)
    token_of = (jnp.arange(row_total, dtype=jnp.int32) // TOP).astype(jnp.int32)
    expert_ids = jnp.arange(EXPERTS, dtype=jnp.int32)

    def expert_rows(expert):
        picked = jnp.nonzero(flat_routes == expert, size=slot_count, fill_value=row_total)[0].astype(jnp.int32)
        live_rows = picked < row_total
        safe_rows = jnp.minimum(picked, row_total - 1).astype(jnp.int32)
        owners = token_of[safe_rows]
        x_rows = jnp.where(live_rows[:, None], flat_acts[owners], jnp.zeros((), acts.dtype))
        selected = latent_mask(flat_index[safe_rows], F) & live_rows[:, None]
        return (picked, live_rows, owners, x_rows, selected)

    def forward(expert):
        picked, live_rows, owners, x_rows, selected = expert_rows(expert)
        preact = jnp.dot(x_rows, enc_weight[expert].reshape(inner_width, F), preferred_element_type=jnp.float32) + enc_bias[expert]
        activated = jax.nn.silu(preact).astype(jnp.bfloat16)
        latent = jnp.where(selected, activated, jnp.zeros((), jnp.bfloat16))
        decoded = jnp.dot(latent, dec_weight[expert].reshape(F, inner_width), preferred_element_type=jnp.float32).astype(jnp.bfloat16)
        return (decoded, picked, preact, latent)
    decoded_all, picked_all, preact_all, latent_all = lax.map(forward, expert_ids)
    rebuilt = jnp.zeros((row_total, inner_width), jnp.bfloat16)
    rebuilt = rebuilt.at[picked_all.reshape(-1)].set(decoded_all.reshape(-1, inner_width), mode='drop')
    total = rebuilt.astype(jnp.float32).reshape(TOKENS, TOP, inner_width).sum(axis=1)
    total = total + dec_bias.reshape(inner_width).astype(jnp.float32)
    residual = (total - flat_acts.astype(jnp.float32)).astype(jnp.bfloat16)

    def backward(packed):
        expert, preact, latent = packed
        picked, live_rows, owners, x_rows, selected = expert_rows(expert)
        res_rows = jnp.where(live_rows[:, None], residual[owners], jnp.zeros((), jnp.bfloat16))
        dec_matrix = dec_weight[expert].reshape(F, inner_width)
        grad_dec = jnp.dot(latent.T, res_rows, preferred_element_type=jnp.float32).astype(jnp.bfloat16)
        latent_grad = jnp.dot(res_rows, dec_matrix.T, preferred_element_type=jnp.float32)
        slope = (latent_grad * silu_grad(preact)).astype(jnp.bfloat16)
        pre_grad = jnp.where(selected, slope, jnp.zeros((), jnp.bfloat16))
        grad_enc = (jnp.dot(x_rows.T, pre_grad, preferred_element_type=jnp.float32) * scale_factor).astype(jnp.bfloat16)
        return (grad_enc, grad_dec)
    grad_enc, grad_dec = lax.map(backward, (expert_ids, preact_all, latent_all))
    return (grad_enc.reshape(EXPERTS, L, D, F), grad_dec.reshape(EXPERTS, F, L, D))
```

```python
import functools
import math

import jax
import jax.numpy as jnp
from jax import lax
from jax.experimental import pallas as pl
from jax.experimental.pallas import tpu as pltpu
from jax.sharding import PartitionSpec as P

D = 8192
L = 2
CAP = 64
GROUPS = 16
CHUNKS = (32, 32)
LANES = 128
KEPT = 32
PER = LANES // KEPT
BF16 = jnp.bfloat16
F32 = jnp.float32
I32 = jnp.int32
ROW_BLOCK = 256
VMEM_LIMIT = 48 * 1024 * 1024


def iota(shape, dim):
    return lax.broadcasted_iota(I32, shape, dim)


def params():
    return pltpu.CompilerParams(vmem_limit_bytes=VMEM_LIMIT)


def cost(flops, nbytes):
    return pl.CostEstimate(flops=int(flops), bytes_accessed=int(nbytes), transcendentals=0)


def whole():
    return pl.BlockSpec(memory_space=pltpu.VMEM)


def offsets():
    out, start = [], 0
    for cap in CHUNKS:
        out.append((start, cap))
        start += cap
    return out


def chunk_hits(info, off, cap, tokens):
    rows = iota((GROUPS * cap, tokens), 0)

    def slot(route, pos):
        inside = (pos >= off) & (pos < off + cap)
        return jnp.where(inside, route * cap + (pos - off), -1)

    return (rows == slot(info[0:1], info[1:2])) | (rows == slot(info[2:3], info[3:4]))


def pack_kernel(routes_ref, acts_ref, info_ref, *send_refs):
    tokens = routes_ref.shape[1]
    upper = (iota((tokens, tokens), 0) < iota((tokens, tokens), 1)).astype(F32).astype(BF16)
    experts = iota((GROUPS, tokens), 0)
    total = jnp.zeros((GROUPS, 1), F32)
    rows = []
    for j in range(2):
        route = routes_ref[j : j + 1, :]
        hit = experts == route
        hot = hit.astype(F32)
        before = jnp.dot(hot.astype(BF16), upper, preferred_element_type=F32) + total
        total = total + jnp.sum(hot, axis=1, keepdims=True)
        pos = jnp.sum(jnp.where(hit, before, 0.0), axis=0, keepdims=True).astype(I32)
        rows += [route, pos]
    info = jnp.concatenate(rows + [jnp.zeros((4, tokens), I32)], axis=0)
    info_ref[...] = info
    x = acts_ref[...]
    for (off, cap), send_ref in zip(offsets(), send_refs):
        hits = chunk_hits(info, off, cap, tokens).astype(F32).astype(BF16)
        send_ref[...] = jnp.dot(hits, x, preferred_element_type=F32).astype(BF16)


def pack(routes_t, x):
    tokens, width = x.shape
    return pl.pallas_call(
        pack_kernel,
        out_shape=(jax.ShapeDtypeStruct((8, tokens), I32),)
        + tuple(jax.ShapeDtypeStruct((GROUPS * c, width), BF16) for c in CHUNKS),
        in_specs=[whole(), whole()],
        out_specs=(whole(),) * (1 + len(CHUNKS)),
        compiler_params=params(),
        cost_estimate=cost(2 * GROUPS * CAP * tokens * width, 3 << 20),
        name="pack_tokens",
    )(routes_t, x)


def index_kernel(info_ref, index_ref, out_ref):
    tokens, cols = index_ref.shape
    index = index_ref[...]
    code = (((index & 127) + 128) << (index >> 7)).astype(F32).astype(BF16)
    info = info_ref[...]
    col = iota((cols, LANES), 0)
    lane = iota((cols, LANES), 1)
    rows_total = GROUPS * CAP // PER
    row = iota((rows_total, tokens), 0)
    per_group = CAP // PER
    expert, inner = row // per_group, row % per_group
    lane_q = iota((rows_total, LANES), 1) // KEPT
    result = jnp.zeros((rows_total, LANES), F32)
    for j in range(2):
        spread = (col == j * KEPT + lane % KEPT).astype(F32).astype(BF16)
        codes = jnp.dot(code, spread, preferred_element_type=F32).astype(BF16)
        key = info[2 * j : 2 * j + 1] * CAP + info[2 * j + 1 : 2 * j + 2]
        for q in range(PER):
            pos = jnp.zeros((rows_total, tokens), I32)
            for off, cap in offsets():
                here = (inner >= off // PER) & (inner < (off + cap) // PER)
                pos = jnp.where(here, off + (cap // PER) * q + inner - off // PER, pos)
            hit = (expert * CAP + pos == key).astype(F32).astype(BF16)
            picked = jnp.dot(hit, codes, preferred_element_type=F32)
            result = result + jnp.where(lane_q == q, picked, 0.0)
    out_ref[...] = result.astype(BF16)


def pack_index(info, index):
    return pl.pallas_call(
        index_kernel,
        out_shape=jax.ShapeDtypeStruct((GROUPS * CAP // PER, LANES), BF16),
        in_specs=[whole(), whole()],
        out_specs=whole(),
        compiler_params=params(),
        cost_estimate=cost(2 * 8 * 256 * 256 * 128, 1 << 18),
        name="pack_index",
    )(info, index)


def inverse_kernel(index_ref, low_ref, high_ref):
    packed_rows = index_ref.shape[1]
    lane = iota((8, LANES), 1)

    def step(g, carry):
        src = g // (packed_rows // 8)
        half = g % (packed_rows // 8)
        idx = index_ref[src, pl.ds(pl.multiple_of(half * 8, 8), 8), :]
        tile = idx >> 7
        low_word = jnp.where((tile >= 0) & (tile < 4), 1 << (jnp.clip(tile, 0, 3) * 6), 0)
        high_word = jnp.where(tile >= 4, 1 << (jnp.clip(tile - 4, 0, 3) * 6), 0)
        place = jnp.where(idx >= 0, idx & 127, -1)
        for q in range(PER):
            low = jnp.zeros((8, LANES), I32)
            high = jnp.zeros((8, LANES), I32)
            for k in range(KEPT):
                c = q * KEPT + k
                same = lane == place[:, c : c + 1]
                low = low + jnp.where(same, low_word[:, c : c + 1] * (k + 1), 0)
                high = high + jnp.where(same, high_word[:, c : c + 1] * (k + 1), 0)
            row = src * (packed_rows * PER) + q * packed_rows + half * 8
            row = pl.multiple_of(row, 8)
            low_ref[pl.ds(row, 8), :] = low
            high_ref[pl.ds(row, 8), :] = high
        return carry

    lax.fori_loop(0, GROUPS * packed_rows // 8, step, 0)


def inverse(index):
    rows = index.shape[0] * index.shape[1] * PER
    shape = jax.ShapeDtypeStruct((rows, LANES), I32)
    return pl.pallas_call(
        inverse_kernel,
        out_shape=(shape, shape),
        in_specs=[whole()],
        out_specs=(whole(), whole()),
        compiler_params=params(),
        cost_estimate=cost(rows * 2_000_000, 1 << 20),
        name="inverse_index",
    )(index)


def gather_kept(values_ref, index_ref, out_ref, groups, packed_rows):
    tiles = values_ref.shape[1] // LANES
    lane_q = iota((8, LANES), 1) // KEPT
    for src in range(groups):
        for half in range(packed_rows // 8):
            idx = index_ref[src, half * 8 : half * 8 + 8, :]
            spot, tile = idx & 127, idx >> 7
            result = jnp.zeros((8, LANES), F32)
            for q in range(PER):
                row = src * packed_rows * PER + q * packed_rows + half * 8
                here = jnp.where(lane_q == q, tile, -1)
                for t in range(tiles):
                    part = values_ref[row : row + 8, t * LANES : (t + 1) * LANES]
                    taken = jnp.take_along_axis(part, spot, axis=1, mode="promise_in_bounds")
                    result = jnp.where(here == t, taken, result)
            start = src * packed_rows + half * 8
            out_ref[start : start + 8, :] = result


def encode_kernel(x_ref, w_ref, bias_ref, index_ref, out_ref, values_ref):
    values_ref[...] = jnp.dot(x_ref[...], w_ref[...], preferred_element_type=F32) + bias_ref[...]
    gather_kept(values_ref, index_ref, out_ref, index_ref.shape[0], index_ref.shape[1])


def backproject_kernel(r_ref, w_ref, index_ref, out_ref, values_ref):
    values_ref[...] = lax.dot_general(
        r_ref[...], w_ref[...], (((1,), (1,)), ((), ())), preferred_element_type=F32
    )
    gather_kept(values_ref, index_ref, out_ref, index_ref.shape[0], index_ref.shape[1])


def kept_product(kernel, rows, weight, index, bias, name):
    total, inner = rows.shape
    latents = 1024
    packed_rows = index.shape[1]
    groups = ROW_BLOCK // (packed_rows * PER)
    operands = [rows, weight] + ([] if bias is None else [bias]) + [index]
    specs = [
        pl.BlockSpec((ROW_BLOCK, inner), lambda i: (i, 0)),
        pl.BlockSpec(weight.shape, lambda i: (0, 0)),
    ]
    if bias is not None:
        specs.append(pl.BlockSpec(bias.shape, lambda i: (0, 0)))
    specs.append(pl.BlockSpec((groups, packed_rows, LANES), lambda i: (i, 0, 0)))
    return pl.pallas_call(
        kernel,
        grid=(total // ROW_BLOCK,),
        out_shape=jax.ShapeDtypeStruct((total // PER, LANES), F32),
        in_specs=specs,
        out_specs=pl.BlockSpec((ROW_BLOCK // PER, LANES), lambda i: (i, 0)),
        scratch_shapes=[pltpu.VMEM((ROW_BLOCK, latents), F32)],
        compiler_params=params(),
        cost_estimate=cost(4 * total * inner * latents, 4 << 20),
        name=name,
    )(*operands)


def spread_kept(kept_ref, low_ref, high_ref, dense_ref, groups, packed_rows):
    for src in range(groups):
        for half in range(packed_rows // 8):
            start = src * packed_rows + half * 8
            kept = kept_ref[start : start + 8, :]
            for q in range(PER):
                row = src * packed_rows * PER + q * packed_rows + half * 8
                words = (low_ref[row : row + 8, :], high_ref[row : row + 8, :])
                for t in range(8):
                    place = (words[t // 4] >> (6 * (t % 4))) & 63
                    spot = jnp.maximum(place - 1, 0) + q * KEPT
                    taken = jnp.take_along_axis(kept, spot, axis=1, mode="promise_in_bounds")
                    dense_ref[row : row + 8, t * LANES : (t + 1) * LANES] = jnp.where(
                        place > 0, taken, 0.0
                    )


def decode_kernel(packed_rows, pre_ref, low_ref, high_ref, w_ref, latent_ref, out_ref, kept_ref, dense_ref):
    pre = pre_ref[...]
    kept_ref[...] = (pre / (1.0 + jnp.exp(-pre))).astype(BF16).astype(F32)
    spread_kept(kept_ref, low_ref, high_ref, dense_ref, ROW_BLOCK // (packed_rows * PER), packed_rows)
    latent = dense_ref[...].astype(BF16)
    latent_ref[...] = latent
    out_ref[...] = jnp.dot(latent, w_ref[...], preferred_element_type=F32).astype(BF16)


def decode(pre, low, high, weight, packed_rows):
    total = low.shape[0]
    latents, inner = weight.shape
    by_row = lambda i: (i, 0)
    return pl.pallas_call(
        functools.partial(decode_kernel, packed_rows),
        grid=(total // ROW_BLOCK,),
        out_shape=(
            jax.ShapeDtypeStruct((total, latents), BF16),
            jax.ShapeDtypeStruct((total, inner), BF16),
        ),
        in_specs=[
            pl.BlockSpec((ROW_BLOCK // PER, LANES), by_row),
            pl.BlockSpec((ROW_BLOCK, LANES), by_row),
            pl.BlockSpec((ROW_BLOCK, LANES), by_row),
            pl.BlockSpec(weight.shape, lambda i: (0, 0)),
        ],
        out_specs=(
            pl.BlockSpec((ROW_BLOCK, latents), by_row),
            pl.BlockSpec((ROW_BLOCK, inner), by_row),
        ),
        scratch_shapes=[
            pltpu.VMEM((ROW_BLOCK // PER, LANES), F32),
            pltpu.VMEM((ROW_BLOCK, latents), F32),
        ],
        compiler_params=params(),
        cost_estimate=cost(4 * total * inner * latents, 6 << 20),
        name="decode",
    )(pre, low, high, weight)


def residual_kernel(*refs):
    count = len(CHUNKS)
    info_ref, x_ref, bias_ref = refs[:3]
    back_refs, send_refs = refs[3 : 3 + count], refs[3 + count :]
    tokens = x_ref.shape[0]
    info = info_ref[...]
    hits = [chunk_hits(info, off, cap, tokens).astype(F32).astype(BF16) for off, cap in offsets()]
    total = jnp.zeros(x_ref.shape, F32)
    for hit, back_ref in zip(hits, back_refs):
        total = total + lax.dot_general(
            hit, back_ref[...], (((0,), (0,)), ((), ())), preferred_element_type=F32
        )
    residual = (total + bias_ref[...] - x_ref[...].astype(F32)).astype(BF16)
    for hit, send_ref in zip(hits, send_refs):
        send_ref[...] = jnp.dot(hit, residual, preferred_element_type=F32).astype(BF16)


def form_residual(info, x, bias, back):
    tokens, width = x.shape
    return pl.pallas_call(
        residual_kernel,
        out_shape=tuple(jax.ShapeDtypeStruct((GROUPS * c, width), BF16) for c in CHUNKS),
        in_specs=[whole()] * (3 + len(CHUNKS)),
        out_specs=(whole(),) * len(CHUNKS),
        compiler_params=params(),
        cost_estimate=cost(4 * GROUPS * CAP * tokens * width, 5 << 20),
        name="form_residual",
    )(info, x, bias, *back)


def encoder_grad_kernel(chunk, scale, first, lg_ref, pre_ref, low_ref, high_ref, xt_ref, out_ref, kept_ref, dense_ref, acc_ref):
    step = pl.program_id(0)
    pre = pre_ref[...]
    sig = 1.0 / (1.0 + jnp.exp(-pre))
    slope = lg_ref[...] * (sig * (1.0 + pre * (1.0 - sig)))
    kept_ref[...] = slope.astype(BF16).astype(F32)
    packed_rows = chunk // PER
    spread_kept(kept_ref, low_ref, high_ref, dense_ref, ROW_BLOCK // chunk, packed_rows)
    part = jnp.dot(xt_ref[...], dense_ref[...].astype(BF16), preferred_element_type=F32)

    @pl.when(step == 0)
    def _():
        acc_ref[...] = part

    @pl.when(step > 0)
    def _():
        acc_ref[...] += part

    @pl.when(step == pl.num_programs(0) - 1)
    def _():
        out_ref[...] = (acc_ref[...] * scale).astype(BF16)


def encoder_grad(lg, pre, low, high, x_t, chunk, scale):
    total = low.shape[0]
    inner, latents = x_t.shape[0], 1024
    by_row = lambda i: (i, 0)
    return pl.pallas_call(
        functools.partial(encoder_grad_kernel, chunk, scale, 0),
        grid=(total // ROW_BLOCK,),
        out_shape=jax.ShapeDtypeStruct((inner, latents), BF16),
        in_specs=[
            pl.BlockSpec((ROW_BLOCK // PER, LANES), by_row),
            pl.BlockSpec((ROW_BLOCK // PER, LANES), by_row),
            pl.BlockSpec((ROW_BLOCK, LANES), by_row),
            pl.BlockSpec((ROW_BLOCK, LANES), by_row),
            pl.BlockSpec((inner, ROW_BLOCK), lambda i: (0, i)),
        ],
        out_specs=pl.BlockSpec((inner, latents), lambda i: (0, 0)),
        scratch_shapes=[
            pltpu.VMEM((ROW_BLOCK // PER, LANES), F32),
            pltpu.VMEM((ROW_BLOCK, latents), F32),
            pltpu.VMEM((inner, latents), F32),
        ],
        compiler_params=params(),
        cost_estimate=cost(4 * total * inner * latents, 6 << 20),
        name="encoder_grad",
    )(lg, pre, low, high, x_t)


def exchange(rows):
    count, width = rows.shape
    return lax.all_to_all(
        rows.reshape(GROUPS, count // GROUPS, width), "feat", split_axis=0, concat_axis=0, tiled=True
    ).reshape(count, width)


def width_sum(part):
    size = lax.axis_size("width")
    bit = 1
    while bit < size:
        part = part + lax.ppermute(part, "width", [(a, a ^ bit) for a in range(size)])
        bit *= 2
    return part


def decode_index(codes):
    code = codes.astype(F32).astype(I32)
    tile = sum((code >= (256 << h)).astype(I32) for h in range(7))
    spot = (code >> tile) - 128
    return jnp.where(code > 0, tile * 128 + spot, -1)


def per_device(acts, enc_weight, enc_bias, dec_weight, dec_bias, routes, latent_index):
    tokens, layers, width_dev = acts.shape
    inner = layers * width_dev
    latents = enc_weight.shape[3]
    scale = 1.0 / math.sqrt(L * D)
    x_home = acts.reshape(tokens, inner)
    enc = enc_weight.reshape(inner, latents)
    dec = dec_weight.reshape(latents, inner)
    bias = jnp.where(lax.axis_index("width") == 0, enc_bias, 0.0)

    info, *sends = pack(routes.T, x_home)
    arrived = [exchange(sends[0])]
    codes = pack_index(info, latent_index.reshape(tokens, 2 * KEPT))
    index = decode_index(exchange(codes)).reshape(GROUPS, CAP // PER, LANES)
    arrived += [exchange(s) for s in sends[1:]]
    index_of = [index[:, off // PER : (off + cap) // PER] for off, cap in offsets()]
    maps = [inverse(i) for i in index_of]

    pre, latent, back = [], [], []
    for c, cap in enumerate(CHUNKS):
        part = kept_product(encode_kernel, arrived[c], enc, index_of[c], bias, "encode")
        pre.append(width_sum(part))
        lat, decoded = decode(pre[c], *maps[c], dec, cap // PER)
        latent.append(lat)
        back.append(exchange(decoded))

    outgoing = form_residual(info, x_home, dec_bias.reshape(1, inner), back)
    res = [exchange(o) for o in outgoing]
    slopes = []
    for c in range(len(CHUNKS)):
        part = kept_product(backproject_kernel, res[c], dec, index_of[c], None, "latent_gradient")
        slopes.append(width_sum(part))
    grad_dec = lax.dot_general(
        jnp.concatenate(latent, axis=0),
        jnp.concatenate(res, axis=0),
        (((0,), (0,)), ((), ())),
        preferred_element_type=F32,
    ).astype(BF16)
    x_t = jnp.concatenate(arrived, axis=0).T
    grad_enc = encoder_grad(
        jnp.concatenate(slopes, axis=0),
        jnp.concatenate(pre, axis=0),
        jnp.concatenate([m[0] for m in maps], axis=0),
        jnp.concatenate([m[1] for m in maps], axis=0),
        x_t,
        CHUNKS[0],
        scale,
    )
    return (
        grad_enc.reshape(1, layers, width_dev, latents),
        grad_dec.reshape(1, latents, layers, width_dev),
    )


def solution(mesh):
    placed = (
        P("feat", None, "width"),
        P("feat", None, "width", None),
        P("feat", None),
        P("feat", None, None, "width"),
        P(None, "width"),
        P("feat", None),
        P("feat", None, None),
    )
    return jax.shard_map(
        per_device,
        mesh=mesh,
        in_specs=placed,
        out_specs=(P("feat", None, "width", None), P("feat", None, None, "width")),
        check_vma=False,
    )
```

```python
import functools
import math

import jax
import jax.numpy as jnp
from jax import lax
from jax.experimental import pallas as pl
from jax.experimental.pallas import tpu as pltpu
from jax.sharding import PartitionSpec as P

D = 8192
L = 2
CAP = 64
GROUPS = 16
CHUNKS = (32, 32)
LANES = 128
KEPT = 32
PER = LANES // KEPT
BF16 = jnp.bfloat16
F32 = jnp.float32
I32 = jnp.int32
ROW_BLOCK = 256
VMEM_LIMIT = 20 * 1024 * 1024


def iota(shape, dim):
    return lax.broadcasted_iota(I32, shape, dim)


def params():
    return pltpu.CompilerParams(vmem_limit_bytes=VMEM_LIMIT)


def cost(flops, nbytes):
    return pl.CostEstimate(flops=int(flops), bytes_accessed=int(nbytes), transcendentals=0)


def whole():
    return pl.BlockSpec(memory_space=pltpu.VMEM)


def offsets():
    out, start = [], 0
    for cap in CHUNKS:
        out.append((start, cap))
        start += cap
    return out


def chunk_hits(info, off, cap, tokens):
    rows = iota((GROUPS * cap, tokens), 0)

    def slot(route, pos):
        inside = (pos >= off) & (pos < off + cap)
        return jnp.where(inside, route * cap + (pos - off), -1)

    return (rows == slot(info[0:1], info[1:2])) | (rows == slot(info[2:3], info[3:4]))


def pack_kernel(routes_ref, acts_ref, index_ref, info_ref, *send_refs):
    tokens, inner = acts_ref.shape
    upper = (iota((tokens, tokens), 0) < iota((tokens, tokens), 1)).astype(F32).astype(BF16)
    experts = iota((GROUPS, tokens), 0)
    total = jnp.zeros((GROUPS, 1), F32)
    rows = []
    for j in range(2):
        route = routes_ref[j : j + 1, :]
        hit = experts == route
        hot = hit.astype(F32)
        before = jnp.dot(hot.astype(BF16), upper, preferred_element_type=F32) + total
        total = total + jnp.sum(hot, axis=1, keepdims=True)
        pos = jnp.sum(jnp.where(hit, before, 0.0), axis=0, keepdims=True).astype(I32)
        rows += [route, pos]
    info = jnp.concatenate(rows + [jnp.zeros((4, tokens), I32)], axis=0)
    info_ref[...] = info
    x = acts_ref[...]
    for (off, cap), send_ref in zip(offsets(), send_refs):
        hits = chunk_hits(info, off, cap, tokens).astype(F32).astype(BF16)
        send_ref[:, :inner] = jnp.dot(hits, x, preferred_element_type=F32).astype(BF16)
    send_refs[0][:, inner:] = index_codes(info, index_ref[...])


def index_codes(info, index):
    tokens, cols = index.shape
    code = (((index & 127) + 128) << (index >> 7)).astype(F32).astype(BF16)
    col = iota((cols, LANES), 0)
    lane = iota((cols, LANES), 1)
    first = CHUNKS[0]
    rows_total = GROUPS * first
    row = iota((rows_total, tokens), 0)
    expert, inner = row // first, row % first
    base = jnp.full((rows_total, tokens), -(1 << 20), I32)
    step = jnp.zeros((rows_total, tokens), I32)
    for off, cap in offsets():
        here = (inner >= off // PER) & (inner < (off + cap) // PER)
        base = jnp.where(here, expert * CAP + off + inner - off // PER, base)
        step = jnp.where(here, cap // PER, step)
    lane_q = iota((rows_total, LANES), 1) // KEPT
    result = jnp.zeros((rows_total, LANES), F32)
    for j in range(2):
        spread = (col == j * KEPT + lane % KEPT).astype(F32).astype(BF16)
        codes = jnp.dot(code, spread, preferred_element_type=F32).astype(BF16)
        key = info[2 * j : 2 * j + 1] * CAP + info[2 * j + 1 : 2 * j + 2]
        for q in range(PER):
            hit = (base + step * q == key).astype(F32).astype(BF16)
            picked = jnp.dot(hit, codes, preferred_element_type=F32)
            result = result + jnp.where(lane_q == q, picked, 0.0)
    return result.astype(BF16)


def pack(routes_t, x, index):
    tokens, width = x.shape
    widths = [width + LANES] + [width] * (len(CHUNKS) - 1)
    return pl.pallas_call(
        pack_kernel,
        out_shape=(jax.ShapeDtypeStruct((8, tokens), I32),)
        + tuple(jax.ShapeDtypeStruct((GROUPS * c, w), BF16) for c, w in zip(CHUNKS, widths)),
        in_specs=[whole()] * 3,
        out_specs=(whole(),) * (1 + len(CHUNKS)),
        compiler_params=params(),
        cost_estimate=cost(2 * GROUPS * CAP * tokens * width, 3 << 20),
        name="pack_tokens",
    )(routes_t, x, index)


def maps_kernel(codes_ref, *refs):
    scratch_ref = refs[-1]
    first = CHUNKS[0]
    code = codes_ref[...].astype(F32).astype(I32)
    tile = jnp.zeros(code.shape, I32)
    for h in range(7):
        tile = tile + jnp.where(code >= (256 << h), 1, 0)
    numbers = jnp.where(code > 0, tile * 128 + (code >> tile) - 128, -1)
    for c, (off, cap) in enumerate(offsets()):
        index_ref, low_ref, high_ref = refs[3 * c : 3 * c + 3]
        packed = cap // PER
        rows = [
            numbers[src * first + off // PER : src * first + (off + cap) // PER] for src in range(GROUPS)
        ]
        idx = jnp.concatenate(rows, axis=0)
        for src in range(GROUPS):
            index_ref[src] = rows[src]
        turned = idx.T
        tile = turned >> 7
        scratch_ref[0] = jnp.where(turned >= 0, turned & 127, -1)
        place = (iota(turned.shape, 0) % KEPT) + 1
        scratch_ref[1] = jnp.where((tile >= 0) & (tile < 4), place << (jnp.clip(tile, 0, 3) * 6), 0)
        scratch_ref[2] = jnp.where(tile >= 4, place << (jnp.clip(tile - 4, 0, 3) * 6), 0)
        for q in range(PER):
            lows, highs = [], []
            for part in range(2):
                size = LANES // 2
                spot = iota((size, LANES), 0) + part * size
                low = jnp.zeros((size, LANES), I32)
                high = jnp.zeros((size, LANES), I32)
                for k in range(KEPT):
                    at = q * KEPT + k
                    same = spot == scratch_ref[0, at : at + 1, :]
                    low = low + jnp.where(same, scratch_ref[1, at : at + 1, :], 0)
                    high = high + jnp.where(same, scratch_ref[2, at : at + 1, :], 0)
                lows.append(low)
                highs.append(high)
            low = jnp.concatenate(lows, axis=0).T
            high = jnp.concatenate(highs, axis=0).T
            for src in range(GROUPS):
                row = src * cap + q * packed
                low_ref[row : row + packed, :] = low[src * packed : (src + 1) * packed]
                high_ref[row : row + packed, :] = high[src * packed : (src + 1) * packed]


def slot_maps(arrived):
    rows, width = arrived.shape
    shapes = []
    for cap in CHUNKS:
        shapes.append(jax.ShapeDtypeStruct((GROUPS, cap // PER, LANES), I32))
        shapes += [jax.ShapeDtypeStruct((GROUPS * cap, LANES), I32)] * 2
    out = pl.pallas_call(
        maps_kernel,
        grid=(1,),
        out_shape=tuple(shapes),
        in_specs=[pl.BlockSpec((rows, LANES), lambda i: (0, width // LANES - 1))],
        out_specs=tuple(
            pl.BlockSpec(s.shape, functools.partial(lambda n, i: (0,) * n, len(s.shape))) for s in shapes
        ),
        scratch_shapes=[pltpu.VMEM((3, LANES, LANES), I32)],
        compiler_params=params(),
        cost_estimate=cost(4_000_000_000, 1 << 20),
        name="slot_maps",
    )(arrived)
    return [out[3 * c : 3 * c + 3] for c in range(len(CHUNKS))]


def skipping(kernel, inputs, extra):
    def run(*refs):
        kernel(*refs[:inputs], *refs[inputs + extra :])

    return run


TOKEN = jax.ShapeDtypeStruct((8, LANES), F32)


def token_spec():
    return pl.BlockSpec((8, LANES), lambda *i: (0, 0))


def gather_kept(values_ref, index_ref, out_ref, groups, packed_rows):
    tiles = values_ref.shape[1] // LANES
    lane_q = iota((8, LANES), 1) // KEPT
    for src in range(groups):
        for half in range(packed_rows // 8):
            idx = index_ref[src, half * 8 : half * 8 + 8, :]
            spot, tile = idx & 127, idx >> 7
            result = jnp.zeros((8, LANES), F32)
            for q in range(PER):
                row = src * packed_rows * PER + q * packed_rows + half * 8
                here = jnp.where(lane_q == q, tile, -1)
                for t in range(tiles):
                    part = values_ref[row : row + 8, t * LANES : (t + 1) * LANES]
                    taken = jnp.take_along_axis(part, spot, axis=1, mode="promise_in_bounds")
                    result = jnp.where(here == t, taken, result)
            start = src * packed_rows + half * 8
            out_ref[start : start + 8, :] = result


def encode_kernel(x_ref, w_ref, bias_ref, index_ref, out_ref, values_ref):
    values_ref[...] = jnp.dot(x_ref[...], w_ref[...], preferred_element_type=F32) + bias_ref[...]
    gather_kept(values_ref, index_ref, out_ref, index_ref.shape[0], index_ref.shape[1])


def backproject_kernel(r_ref, w_ref, index_ref, out_ref, values_ref):
    values_ref[...] = lax.dot_general(
        r_ref[...], w_ref[...], (((1,), (1,)), ((), ())), preferred_element_type=F32
    )
    gather_kept(values_ref, index_ref, out_ref, index_ref.shape[0], index_ref.shape[1])


def kept_product(kernel, rows, weight, index, bias, name, after=()):
    total = rows.shape[0]
    inner, latents = 1024, 1024
    packed_rows = index.shape[1]
    groups = ROW_BLOCK // (packed_rows * PER)
    operands = [rows, weight] + ([] if bias is None else [bias]) + [index]
    specs = [
        pl.BlockSpec((ROW_BLOCK, inner), lambda i: (i, 0)),
        pl.BlockSpec(weight.shape, lambda i: (0, 0)),
    ]
    if bias is not None:
        specs.append(pl.BlockSpec(bias.shape, lambda i: (0, 0)))
    specs.append(pl.BlockSpec((groups, packed_rows, LANES), lambda i: (i, 0, 0)))
    return pl.pallas_call(
        skipping(kernel, len(operands), len(after)),
        grid=(total // ROW_BLOCK,),
        out_shape=jax.ShapeDtypeStruct((total // PER, LANES), F32),
        in_specs=specs + [token_spec()] * len(after),
        out_specs=pl.BlockSpec((ROW_BLOCK // PER, LANES), lambda i: (i, 0)),
        scratch_shapes=[pltpu.VMEM((ROW_BLOCK, latents), F32)],
        compiler_params=params(),
        cost_estimate=cost(4 * total * inner * latents, 4 << 20),
        name=name,
    )(*operands, *after)


def spread_kept(kept_ref, low_ref, high_ref, dense_ref, groups, packed_rows):
    for src in range(groups):
        for half in range(packed_rows // 8):
            start = src * packed_rows + half * 8
            kept = kept_ref[start : start + 8, :]
            for q in range(PER):
                row = src * packed_rows * PER + q * packed_rows + half * 8
                words = (low_ref[row : row + 8, :], high_ref[row : row + 8, :])
                for t in range(8):
                    place = (words[t // 4] >> (6 * (t % 4))) & 63
                    spot = jnp.maximum(place - 1, 0) + q * KEPT
                    taken = jnp.take_along_axis(kept, spot, axis=1, mode="promise_in_bounds")
                    dense_ref[row : row + 8, t * LANES : (t + 1) * LANES] = jnp.where(
                        place > 0, taken, 0.0
                    )


def decode_kernel(packed_rows, pre_ref, low_ref, high_ref, w_ref, latent_ref, out_ref, token_ref, kept_ref, dense_ref):
    token_ref[...] = jnp.zeros_like(token_ref)
    pre = pre_ref[...]
    kept_ref[...] = (pre / (1.0 + jnp.exp(-pre))).astype(BF16).astype(F32)
    spread_kept(kept_ref, low_ref, high_ref, dense_ref, ROW_BLOCK // (packed_rows * PER), packed_rows)
    latent = dense_ref[...].astype(BF16)
    latent_ref[...] = latent
    out_ref[...] = jnp.dot(latent, w_ref[...], preferred_element_type=F32).astype(BF16)


def decode(pre, low, high, weight, packed_rows):
    total = low.shape[0]
    latents, inner = weight.shape
    by_row = lambda i: (i, 0)
    return pl.pallas_call(
        functools.partial(decode_kernel, packed_rows),
        grid=(total // ROW_BLOCK,),
        out_shape=(
            jax.ShapeDtypeStruct((total, latents), BF16),
            jax.ShapeDtypeStruct((total, inner), BF16),
            TOKEN,
        ),
        in_specs=[
            pl.BlockSpec((ROW_BLOCK // PER, LANES), by_row),
            pl.BlockSpec((ROW_BLOCK, LANES), by_row),
            pl.BlockSpec((ROW_BLOCK, LANES), by_row),
            pl.BlockSpec(weight.shape, lambda i: (0, 0)),
        ],
        out_specs=(
            pl.BlockSpec((ROW_BLOCK, latents), by_row),
            pl.BlockSpec((ROW_BLOCK, inner), by_row),
            token_spec(),
        ),
        scratch_shapes=[
            pltpu.VMEM((ROW_BLOCK // PER, LANES), F32),
            pltpu.VMEM((ROW_BLOCK, latents), F32),
        ],
        compiler_params=params(),
        cost_estimate=cost(4 * total * inner * latents, 6 << 20),
        name="decode",
    )(pre, low, high, weight)


def residual_kernel(*refs):
    count = len(CHUNKS)
    info_ref, x_ref, bias_ref = refs[:3]
    back_refs, send_refs = refs[3 : 3 + count], refs[3 + count :]
    tokens = x_ref.shape[0]
    info = info_ref[...]
    hits = [chunk_hits(info, off, cap, tokens).astype(F32).astype(BF16) for off, cap in offsets()]
    total = jnp.zeros(x_ref.shape, F32)
    for hit, back_ref in zip(hits, back_refs):
        total = total + lax.dot_general(
            hit, back_ref[...], (((0,), (0,)), ((), ())), preferred_element_type=F32
        )
    residual = (total + bias_ref[...] - x_ref[...].astype(F32)).astype(BF16)
    for hit, send_ref in zip(hits, send_refs):
        send_ref[...] = jnp.dot(hit, residual, preferred_element_type=F32).astype(BF16)


def form_residual(info, x, bias, back, after):
    tokens, width = x.shape
    return pl.pallas_call(
        skipping(residual_kernel, 3 + len(CHUNKS), len(after)),
        out_shape=tuple(jax.ShapeDtypeStruct((GROUPS * c, width), BF16) for c in CHUNKS),
        in_specs=[whole()] * (3 + len(CHUNKS) + len(after)),
        out_specs=(whole(),) * len(CHUNKS),
        compiler_params=params(),
        cost_estimate=cost(4 * GROUPS * CAP * tokens * width, 5 << 20),
        name="form_residual",
    )(info, x, bias, *back, *after)


def turn_kernel(*refs):
    half = (len(refs) - 1) // 2
    refs[-1][...] = jnp.zeros(refs[-1].shape, F32)
    for src, dst in zip(refs[:half], refs[half:]):
        dst[...] = src[...].T


def turn(arrived, inner):
    return pl.pallas_call(
        turn_kernel,
        grid=(4,),
        out_shape=tuple(jax.ShapeDtypeStruct((inner, a.shape[0]), BF16) for a in arrived) + (TOKEN,),
        in_specs=[pl.BlockSpec((a.shape[0], inner // 4), lambda i: (0, i)) for a in arrived],
        out_specs=tuple(pl.BlockSpec((inner // 4, a.shape[0]), lambda i: (i, 0)) for a in arrived)
        + (token_spec(),),
        compiler_params=params(),
        cost_estimate=cost(4_000_000_000, 4 << 20),
        name="turn_rows",
    )(*arrived)


def encoder_grad_kernel(chunk, scale, *refs):
    lg_ref, pre_ref, low_ref, high_ref, xt_ref = refs[:5]
    if scale is None:
        out_ref, token_ref, kept_ref, dense_ref, grad_ref = refs[5:]
        token_ref[...] = jnp.zeros_like(token_ref)
    else:
        part_ref, out_ref, kept_ref, dense_ref, grad_ref = refs[5:]

    @pl.when(pl.program_id(0) == 0)
    def _():
        pre = pre_ref[...]
        sig = 1.0 / (1.0 + jnp.exp(-pre))
        slope = lg_ref[...] * (sig * (1.0 + pre * (1.0 - sig)))
        kept_ref[...] = slope.astype(BF16).astype(F32)
        spread_kept(kept_ref, low_ref, high_ref, dense_ref, GROUPS, chunk // PER)
        grad_ref[...] = dense_ref[...].astype(BF16)

    part = jnp.dot(xt_ref[...], grad_ref[...], preferred_element_type=F32)
    if scale is None:
        out_ref[...] = part
    else:
        out_ref[...] = ((part + part_ref[...]) * scale).astype(BF16)


def encoder_grad(lg, pre, low, high, x_t, chunk, scale=None, part=None):
    total = low.shape[0]
    inner, latents = x_t.shape[0], 1024
    block = 256
    all_of = lambda a: pl.BlockSpec(a.shape, lambda i: (0, 0))
    by_row = lambda i: (i, 0)
    operands = [lg, pre, low, high, x_t]
    specs = [all_of(a) for a in operands[:4]] + [pl.BlockSpec((block, total), by_row)]
    result = pl.BlockSpec((block, latents), by_row)
    if scale is None:
        shapes = (jax.ShapeDtypeStruct((inner, latents), F32), TOKEN)
        results = (result, token_spec())
    else:
        operands.append(part)
        specs.append(result)
        shapes, results = jax.ShapeDtypeStruct((inner, latents), BF16), result
    return pl.pallas_call(
        functools.partial(encoder_grad_kernel, chunk, scale),
        grid=(inner // block,),
        out_shape=shapes,
        in_specs=specs,
        out_specs=results,
        scratch_shapes=[
            pltpu.VMEM(lg.shape, F32),
            pltpu.VMEM((total, latents), F32),
            pltpu.VMEM((total, latents), BF16),
        ],
        compiler_params=params(),
        cost_estimate=cost(4 * total * inner * latents, 6 << 20),
        name="encoder_grad",
    )(*operands)


def decoder_grad_kernel(last, latent_ref, res_ref, *refs):
    part = lax.dot_general(
        latent_ref[...], res_ref[...], (((0,), (0,)), ((), ())), preferred_element_type=F32
    )
    if last:
        part_ref, out_ref = refs
        out_ref[...] = (part + part_ref[...]).astype(BF16)
    else:
        out_ref, token_ref = refs
        out_ref[...] = part
        token_ref[...] = jnp.zeros_like(token_ref)


def decoder_grad(latent, res, part=None):
    total, latents = latent.shape
    inner = res.shape[1]
    block = 256
    result = pl.BlockSpec((block, inner), lambda i: (i, 0))
    specs = [pl.BlockSpec((total, block), lambda i: (0, i)), pl.BlockSpec(res.shape, lambda i: (0, 0))]
    operands = [latent, res]
    if part is None:
        shapes = (jax.ShapeDtypeStruct((latents, inner), F32), TOKEN)
        results = (result, token_spec())
    else:
        operands.append(part)
        specs.append(result)
        shapes, results = jax.ShapeDtypeStruct((latents, inner), BF16), result
    return pl.pallas_call(
        functools.partial(decoder_grad_kernel, part is not None),
        grid=(latents // block,),
        out_shape=shapes,
        in_specs=specs,
        out_specs=results,
        compiler_params=params(),
        cost_estimate=cost(2 * total * inner * latents, 6 << 20),
        name="decoder_grad",
    )(*operands)


def exchange(rows):
    count, width = rows.shape
    return lax.all_to_all(
        rows.reshape(GROUPS, count // GROUPS, width), "feat", split_axis=0, concat_axis=0, tiled=True
    ).reshape(count, width)


def width_sum(part):
    for masks in ((1,), (2,), (4, 8, 12)):
        size = lax.axis_size("width")
        moved = [lax.ppermute(part, "width", [(a, a ^ m) for a in range(size)]) for m in masks]
        for other in moved:
            part = part + other
    return part


def per_device(acts, enc_weight, enc_bias, dec_weight, dec_bias, routes, latent_index):
    tokens, layers, width_dev = acts.shape
    inner = layers * width_dev
    latents = enc_weight.shape[3]
    scale = 1.0 / math.sqrt(L * D)
    x_home = acts.reshape(tokens, inner)
    enc = enc_weight.reshape(inner, latents)
    dec = dec_weight.reshape(latents, inner)
    bias = jnp.where(lax.axis_index("width") == 0, enc_bias, 0.0)

    info, *sends = pack(routes.T, x_home, latent_index.reshape(tokens, 2 * KEPT))
    arrived = [exchange(s) for s in sends]
    maps = slot_maps(arrived[0])

    pre, latent, back, after = [], [], [], ()
    for c, cap in enumerate(CHUNKS):
        index, low, high = maps[c]
        part = kept_product(encode_kernel, arrived[c], enc, index, bias, "encode", after)
        pre.append(width_sum(part))
        lat, decoded, token = decode(pre[c], low, high, dec, cap // PER)
        after = (token,)
        latent.append(lat)
        back.append(exchange(decoded))

    *turned, token = turn(arrived, inner)
    outgoing = form_residual(info, x_home, dec_bias.reshape(1, inner), back, (token,))
    res = [exchange(o) for o in outgoing]

    def latent_gradient(c, after):
        part = kept_product(backproject_kernel, res[c], dec, maps[c][0], None, "latent_gradient", after)
        return width_sum(part)

    enc_part, enc_token = encoder_grad(
        latent_gradient(0, ()), pre[0], maps[0][1], maps[0][2], turned[0], CHUNKS[0]
    )
    dec_part, dec_token = decoder_grad(latent[0], res[0])
    last = latent_gradient(1, (enc_token, dec_token))
    grad_dec = decoder_grad(latent[1], res[1], dec_part)
    grad_enc = encoder_grad(last, pre[1], maps[1][1], maps[1][2], turned[1], CHUNKS[1], scale, enc_part)
    return (
        grad_enc.reshape(1, layers, width_dev, latents),
        grad_dec.reshape(1, latents, layers, width_dev),
    )


def solution(mesh):
    placed = (
        P("feat", None, "width"),
        P("feat", None, "width", None),
        P("feat", None),
        P("feat", None, None, "width"),
        P(None, "width"),
        P("feat", None),
        P("feat", None, None),
    )
    return jax.shard_map(
        per_device,
        mesh=mesh,
        in_specs=placed,
        out_specs=(P("feat", None, "width", None), P("feat", None, None, "width")),
        check_vma=False,
    )
```

```python
import functools
import math

import jax
import jax.numpy as jnp
from jax import lax
from jax.experimental import pallas as pl
from jax.experimental.pallas import tpu as pltpu
from jax.sharding import PartitionSpec as P

D = 8192
L = 2
CAP = 64
GROUPS = 16
CHUNKS = (32, 32)
LANES = 128
KEPT = 32
PER = LANES // KEPT
BF16 = jnp.bfloat16
F32 = jnp.float32
I32 = jnp.int32
ROW_BLOCK = 256
VMEM_LIMIT = 20 * 1024 * 1024


def iota(shape, dim):
    return lax.broadcasted_iota(I32, shape, dim)


def params():
    return pltpu.CompilerParams(vmem_limit_bytes=VMEM_LIMIT)


def cost(flops, nbytes):
    return pl.CostEstimate(flops=int(flops), bytes_accessed=int(nbytes), transcendentals=0)


def hbm(shape, dtype):
    return pltpu.HBM(shape, dtype)


def vmem(shape, dtype):
    return pltpu.VMEM(shape, dtype)


def in_hbm(x):
    return pltpu.with_memory_space_constraint(x, pltpu.HBM)


def in_vmem(x):
    return pltpu.with_memory_space_constraint(x, pltpu.VMEM)


def whole():
    return pl.BlockSpec(memory_space=pltpu.VMEM)


def offsets():
    out, start = [], 0
    for cap in CHUNKS:
        out.append((start, cap))
        start += cap
    return out


def chunk_hits(info, off, cap, tokens):
    rows = iota((GROUPS * cap, tokens), 0)

    def slot(route, pos):
        inside = (pos >= off) & (pos < off + cap)
        return jnp.where(inside, route * cap + (pos - off), -1)

    return (rows == slot(info[0:1], info[1:2])) | (rows == slot(info[2:3], info[3:4]))


def pack_kernel(routes_ref, acts_ref, index_ref, info_ref, *send_refs):
    tokens, inner = acts_ref.shape
    upper = (iota((tokens, tokens), 0) < iota((tokens, tokens), 1)).astype(F32).astype(BF16)
    experts = iota((GROUPS, tokens), 0)
    total = jnp.zeros((GROUPS, 1), F32)
    rows = []
    for j in range(2):
        route = routes_ref[j : j + 1, :]
        hit = experts == route
        hot = hit.astype(F32)
        before = jnp.dot(hot.astype(BF16), upper, preferred_element_type=F32) + total
        total = total + jnp.sum(hot, axis=1, keepdims=True)
        pos = jnp.sum(jnp.where(hit, before, 0.0), axis=0, keepdims=True).astype(I32)
        rows += [route, pos]
    info = jnp.concatenate(rows + [jnp.zeros((4, tokens), I32)], axis=0)
    info_ref[...] = info
    x = acts_ref[...]
    for (off, cap), send_ref in zip(offsets(), send_refs):
        hits = chunk_hits(info, off, cap, tokens).astype(F32).astype(BF16)
        send_ref[:, :inner] = jnp.dot(hits, x, preferred_element_type=F32).astype(BF16)
    send_refs[0][:, inner:] = index_codes(info, index_ref[...])


def index_codes(info, index):
    tokens, cols = index.shape
    code = (((index & 127) + 128) << (index >> 7)).astype(F32).astype(BF16)
    col = iota((cols, LANES), 0)
    lane = iota((cols, LANES), 1)
    first = CHUNKS[0]
    rows_total = GROUPS * first
    row = iota((rows_total, tokens), 0)
    expert, inner = row // first, row % first
    base = jnp.full((rows_total, tokens), -(1 << 20), I32)
    step = jnp.zeros((rows_total, tokens), I32)
    for off, cap in offsets():
        here = (inner >= off // PER) & (inner < (off + cap) // PER)
        base = jnp.where(here, expert * CAP + off + inner - off // PER, base)
        step = jnp.where(here, cap // PER, step)
    lane_q = iota((rows_total, LANES), 1) // KEPT
    result = jnp.zeros((rows_total, LANES), F32)
    for j in range(2):
        spread = (col == j * KEPT + lane % KEPT).astype(F32).astype(BF16)
        codes = jnp.dot(code, spread, preferred_element_type=F32).astype(BF16)
        key = info[2 * j : 2 * j + 1] * CAP + info[2 * j + 1 : 2 * j + 2]
        for q in range(PER):
            hit = (base + step * q == key).astype(F32).astype(BF16)
            picked = jnp.dot(hit, codes, preferred_element_type=F32)
            result = result + jnp.where(lane_q == q, picked, 0.0)
    return result.astype(BF16)


def pack(routes_t, x, index):
    tokens, width = x.shape
    widths = [width + LANES] + [width] * (len(CHUNKS) - 1)
    return pl.pallas_call(
        pack_kernel,
        out_shape=(jax.ShapeDtypeStruct((8, tokens), I32),)
        + tuple(jax.ShapeDtypeStruct((GROUPS * c, w), BF16) for c, w in zip(CHUNKS, widths)),
        in_specs=[whole()] * 3,
        out_specs=(whole(),) * (1 + len(CHUNKS)),
        compiler_params=params(),
        cost_estimate=cost(2 * GROUPS * CAP * tokens * width, 3 << 20),
        name="pack_tokens",
    )(routes_t, x, index)


def numbers_kernel(codes_ref, *refs):
    first = CHUNKS[0]
    code = codes_ref[...].astype(F32).astype(I32)
    tile = jnp.zeros(code.shape, I32)
    for h in range(7):
        tile = tile + jnp.where(code >= (256 << h), 1, 0)
    numbers = jnp.where(code > 0, tile * 128 + (code >> tile) - 128, -1)
    for (off, cap), index_ref in zip(offsets(), refs):
        for src in range(GROUPS):
            start = src * first + off // PER
            index_ref[src] = numbers[start : start + cap // PER]
    maps_kernel(refs[0], *refs[len(CHUNKS) :])


def maps_kernel(index_ref, low_ref, high_ref, scratch_ref):
    packed = index_ref.shape[1]
    cap = packed * PER
    turned = jnp.concatenate([index_ref[src] for src in range(GROUPS)], axis=0).T
    tile = turned >> 7
    scratch_ref[0] = jnp.where(turned >= 0, turned & 127, -1)
    place = (iota(turned.shape, 0) % KEPT) + 1
    scratch_ref[1] = jnp.where((tile >= 0) & (tile < 4), place << (jnp.clip(tile, 0, 3) * 6), 0)
    scratch_ref[2] = jnp.where(tile >= 4, place << (jnp.clip(tile - 4, 0, 3) * 6), 0)
    for q in range(PER):
        lows, highs = [], []
        for part in range(2):
            size = LANES // 2
            spot = iota((size, LANES), 0) + part * size
            low = jnp.zeros((size, LANES), I32)
            high = jnp.zeros((size, LANES), I32)
            for k in range(KEPT):
                at = q * KEPT + k
                same = spot == scratch_ref[0, at : at + 1, :]
                low = low + jnp.where(same, scratch_ref[1, at : at + 1, :], 0)
                high = high + jnp.where(same, scratch_ref[2, at : at + 1, :], 0)
            lows.append(low)
            highs.append(high)
        low = jnp.concatenate(lows, axis=0).T
        high = jnp.concatenate(highs, axis=0).T
        for src in range(GROUPS):
            row = src * cap + q * packed
            low_ref[row : row + packed, :] = low[src * packed : (src + 1) * packed]
            high_ref[row : row + packed, :] = high[src * packed : (src + 1) * packed]


def map_shapes(cap):
    return [jax.ShapeDtypeStruct((GROUPS * cap, LANES), I32)] * 2


def slot_numbers(arrived):
    rows, width = arrived.shape
    shapes = [jax.ShapeDtypeStruct((GROUPS, cap // PER, LANES), I32) for cap in CHUNKS]
    shapes += map_shapes(CHUNKS[0])
    out = pl.pallas_call(
        numbers_kernel,
        grid=(1,),
        out_shape=tuple(shapes),
        in_specs=[pl.BlockSpec((rows, LANES), lambda i: (0, width // LANES - 1))],
        out_specs=tuple(
            pl.BlockSpec(s.shape, functools.partial(lambda n, i: (0,) * n, len(s.shape))) for s in shapes
        ),
        scratch_shapes=[pltpu.VMEM((3, LANES, LANES), I32)],
        compiler_params=params(),
        cost_estimate=cost(2_000_000_000, 1 << 20),
        name="slot_numbers",
    )(arrived)
    return out[: len(CHUNKS)], [out[len(CHUNKS) :]]


def later_maps_kernel(index_ref, low_ref, high_ref, token_ref, scratch_ref):
    token_ref[...] = jnp.zeros_like(token_ref)
    maps_kernel(index_ref, low_ref, high_ref, scratch_ref)


def slot_maps(index):
    cap = index.shape[1] * PER
    return pl.pallas_call(
        later_maps_kernel,
        out_shape=tuple(map_shapes(cap)) + (TOKEN,),
        in_specs=[whole()],
        out_specs=(whole(),) * 3,
        scratch_shapes=[pltpu.VMEM((3, LANES, LANES), I32)],
        compiler_params=params(),
        cost_estimate=cost(2_000_000_000, 1 << 20),
        name="slot_maps",
    )(index)


def skipping(kernel, inputs, extra):
    def run(*refs):
        kernel(*refs[:inputs], *refs[inputs + extra :])

    return run


TOKEN = jax.ShapeDtypeStruct((8, LANES), F32)


def token_spec():
    return pl.BlockSpec((8, LANES), lambda *i: (0, 0))


def gather_kept(values_ref, index_ref, out_ref, stride, base, start):
    tiles = values_ref.shape[1] // LANES
    packed_rows = index_ref.shape[1]
    lane_q = iota((8, LANES), 1) // KEPT
    for src in range(GROUPS):
        for half in range(packed_rows // 8):
            idx = index_ref[src, half * 8 : half * 8 + 8, :]
            spot, tile = idx & 127, idx >> 7
            result = jnp.zeros((8, LANES), F32)
            for q in range(PER):
                row = src * stride + base + q * packed_rows + half * 8
                here = jnp.where(lane_q == q, tile, -1)
                for t in range(tiles):
                    part = values_ref[row : row + 8, t * LANES : (t + 1) * LANES]
                    taken = jnp.take_along_axis(part, spot, axis=1, mode="promise_in_bounds")
                    result = jnp.where(here == t, taken, result)
            place = start + src * packed_rows + half * 8
            out_ref[place : place + 8, :] = result


def encode_kernel(x_ref, w_ref, bias_ref, index_ref, out_ref, values_ref):
    inner = w_ref.shape[0]
    values_ref[...] = (
        jnp.dot(x_ref[:, :inner], w_ref[...], preferred_element_type=F32) + bias_ref[...]
    )
    gather_kept(values_ref, index_ref, out_ref, index_ref.shape[1] * PER, 0, 0)


def encode(rows, weight, bias, index, after):
    total, latents = rows.shape[0], weight.shape[1]
    return pl.pallas_call(
        skipping(encode_kernel, 4, len(after)),
        out_shape=jax.ShapeDtypeStruct((total // PER, LANES), F32),
        in_specs=[whole()] * (4 + len(after)),
        out_specs=whole(),
        scratch_shapes=[pltpu.VMEM((total, latents), F32)],
        compiler_params=params(),
        cost_estimate=cost(4 * total * 1024 * latents, 4 << 20),
        name="encode",
    )(rows, weight, bias, index, *after)


def latent_gradient_kernel(r_ref, w_ref, *refs):
    index_refs, out_ref, values_ref = refs[:-2], refs[-2], refs[-1]
    values_ref[...] = lax.dot_general(
        r_ref[...], w_ref[...], (((1,), (1,)), ((), ())), preferred_element_type=F32
    )
    start = 0
    for (off, cap), index_ref in zip(offsets(), index_refs):
        gather_kept(values_ref, index_ref, out_ref, CAP, off, start)
        start += GROUPS * cap // PER


def latent_gradient(rows, weight, index):
    total, latents = rows.shape[0], weight.shape[0]
    return pl.pallas_call(
        latent_gradient_kernel,
        out_shape=jax.ShapeDtypeStruct((total // PER, LANES), F32),
        in_specs=[whole()] * (2 + len(index)),
        out_specs=whole(),
        scratch_shapes=[pltpu.VMEM((total, latents), F32)],
        compiler_params=params(),
        cost_estimate=cost(4 * total * 1024 * latents, 4 << 20),
        name="latent_gradient",
    )(rows, weight, *index)


def spread_kept(kept_ref, low_ref, high_ref, dense_ref, groups, packed_rows, source=0, target=0):
    for src in range(groups):
        for q in range(0, PER, 2):
            row = src * packed_rows * PER + q * packed_rows
            kept = kept_ref[src * packed_rows : (src + 1) * packed_rows, :]
            rows = pl.ds(source + row, 2 * packed_rows)
            words = (low_ref[rows, :], high_ref[rows, :])
            kept = jnp.concatenate([kept, kept], axis=0)
            shift = (iota((2 * packed_rows, LANES), 0) // packed_rows + q) * KEPT
            for t in range(8):
                which = (words[t // 4] >> (6 * (t % 4))) & 63
                spot = jnp.maximum(which - 1, 0) + shift
                taken = jnp.take_along_axis(kept, spot, axis=1, mode="promise_in_bounds")
                dense_ref[target + row : target + row + 2 * packed_rows, t * LANES : (t + 1) * LANES] = (
                    jnp.where(which > 0, taken, 0.0).astype(BF16)
                )


def decode_kernel(packed_rows, pre_ref, low_ref, high_ref, w_ref, latent_ref, out_ref, token_ref, kept_ref):
    token_ref[...] = jnp.zeros_like(token_ref)
    pre = pre_ref[...]
    kept_ref[...] = (pre / (1.0 + jnp.exp(-pre))).astype(BF16).astype(F32)
    base = pl.multiple_of(pl.program_id(0) * ROW_BLOCK, ROW_BLOCK)
    groups = ROW_BLOCK // (packed_rows * PER)
    spread_kept(kept_ref, low_ref, high_ref, latent_ref, groups, packed_rows, base)
    out_ref[...] = jnp.dot(latent_ref[...], w_ref[...], preferred_element_type=F32).astype(BF16)


def decode(pre, low, high, weight, packed_rows, after):
    total = low.shape[0]
    latents, inner = weight.shape
    by_row = lambda i: (i, 0)
    return pl.pallas_call(
        skipping(functools.partial(decode_kernel, packed_rows), 4, len(after)),
        grid=(total // ROW_BLOCK,),
        out_shape=(hbm((total, latents), BF16), hbm((total, inner), BF16), TOKEN),
        in_specs=[pl.BlockSpec((ROW_BLOCK // PER, LANES), by_row)] + [whole()] * (3 + len(after)),
        out_specs=(
            pl.BlockSpec((ROW_BLOCK, latents), by_row),
            pl.BlockSpec((ROW_BLOCK, inner), by_row),
            token_spec(),
        ),
        scratch_shapes=[pltpu.VMEM((ROW_BLOCK // PER, LANES), F32)],
        compiler_params=params(),
        cost_estimate=cost(4 * total * inner * latents, 6 << 20),
        name="decode",
    )(pre, low, high, weight, *after)


def residual_kernel(*refs):
    count = len(CHUNKS)
    info_ref, x_ref, bias_ref = refs[:3]
    back_refs, send_ref = refs[3 : 3 + count], refs[3 + count]
    tokens = x_ref.shape[0]
    info = info_ref[...]
    total = jnp.zeros(x_ref.shape, F32)
    for (off, cap), back_ref in zip(offsets(), back_refs):
        hit = chunk_hits(info, off, cap, tokens).astype(F32).astype(BF16)
        total = total + lax.dot_general(
            hit, back_ref[...], (((0,), (0,)), ((), ())), preferred_element_type=F32
        )
    residual = (total + bias_ref[...] - x_ref[...].astype(F32)).astype(BF16)
    hit = chunk_hits(info, 0, CAP, tokens).astype(F32).astype(BF16)
    send_ref[...] = jnp.dot(hit, residual, preferred_element_type=F32).astype(BF16)


def form_residual(info, x, bias, back, after):
    tokens, width = x.shape
    return pl.pallas_call(
        skipping(residual_kernel, 3 + len(CHUNKS), len(after)),
        out_shape=jax.ShapeDtypeStruct((GROUPS * CAP, width), BF16),
        in_specs=[whole()] * (3 + len(CHUNKS) + len(after)),
        out_specs=whole(),
        compiler_params=params(),
        cost_estimate=cost(4 * GROUPS * CAP * tokens * width, 5 << 20),
        name="form_residual",
    )(info, x, bias, *back, *after)


def turn_kernel(*refs):
    half = (len(refs) - 1) // 2
    refs[-1][...] = jnp.zeros(refs[-1].shape, F32)
    for src, dst in zip(refs[:half], refs[half:]):
        block = dst.shape[0]
        here = pl.ds(pl.multiple_of(pl.program_id(0) * block, block), block)
        dst[...] = src[:, here].T


def turn(arrived, inner):
    return pl.pallas_call(
        turn_kernel,
        grid=(4,),
        out_shape=tuple(hbm((inner, a.shape[0]), BF16) for a in arrived) + (TOKEN,),
        in_specs=[whole()] * len(arrived),
        out_specs=tuple(pl.BlockSpec((inner // 4, a.shape[0]), lambda i: (i, 0)) for a in arrived)
        + (token_spec(),),
        compiler_params=params(),
        cost_estimate=cost(4_000_000_000, 4 << 20),
        name="turn_rows",
    )(*arrived)


def encoder_grad_kernel(scale, lg_ref, *refs):
    count = len(CHUNKS)
    pre_refs, map_refs, x_refs = refs[:count], refs[count : 3 * count], refs[3 * count : 4 * count]
    out_ref, grad_ref, kept_ref = refs[4 * count :]

    @pl.when(pl.program_id(0) == 0)
    def _():
        start = 0
        for c, cap in enumerate(CHUNKS):
            packed = GROUPS * cap // PER
            pre = pre_refs[c][...]
            sig = 1.0 / (1.0 + jnp.exp(-pre))
            slope = lg_ref[start : start + packed, :] * (sig * (1.0 + pre * (1.0 - sig)))
            kept_ref[...] = slope.astype(BF16).astype(F32)
            words = map_refs[2 * c : 2 * c + 2]
            spread_kept(kept_ref, *words, grad_ref, GROUPS, cap // PER, 0, start * PER)
            start += packed

    total, start = None, 0
    for c, cap in enumerate(CHUNKS):
        rows = GROUPS * cap
        part = jnp.dot(
            x_refs[c][...], grad_ref[start : start + rows, :], preferred_element_type=F32
        )
        total = part if total is None else total + part
        start += rows
    out_ref[...] = (total * scale).astype(BF16)


def encoder_grad(lg, pre, maps, turned, scale):
    latents = 1024
    inner = turned[0].shape[0]
    block = 256
    rows = GROUPS * CHUNKS[0]
    operands = [lg, *pre, *[m for pair in maps for m in pair]]
    return pl.pallas_call(
        functools.partial(encoder_grad_kernel, scale),
        grid=(inner // block,),
        out_shape=jax.ShapeDtypeStruct((inner, latents), BF16),
        in_specs=[whole()] * len(operands)
        + [pl.BlockSpec((block, t.shape[1]), lambda i: (i, 0)) for t in turned],
        out_specs=pl.BlockSpec((block, latents), lambda i: (i, 0)),
        scratch_shapes=[
            pltpu.VMEM((GROUPS * CAP, latents), BF16),
            pltpu.VMEM((rows // PER, LANES), F32),
        ],
        compiler_params=params(),
        cost_estimate=cost(4 * 1024 * inner * latents, 6 << 20),
        name="encoder_grad",
    )(*operands, *[in_hbm(t) for t in turned])


def decoder_grad_kernel(*refs):
    latent_refs, res_ref, out_ref = refs[:-2], refs[-2], refs[-1]
    block = out_ref.shape[0]
    here = pl.ds(pl.multiple_of(pl.program_id(0) * block, block), block)
    total = None
    for (off, cap), latent_ref in zip(offsets(), latent_refs):
        rows = [res_ref[src * CAP + off : src * CAP + off + cap, :] for src in range(GROUPS)]
        part = lax.dot_general(
            latent_ref[:, here],
            jnp.concatenate(rows, axis=0),
            (((0,), (0,)), ((), ())),
            preferred_element_type=F32,
        )
        total = part if total is None else total + part
    out_ref[...] = total.astype(BF16)


def decoder_grad(latent, res):
    latents, inner = latent[0].shape[1], res.shape[1]
    block = 256
    return pl.pallas_call(
        decoder_grad_kernel,
        grid=(latents // block,),
        out_shape=jax.ShapeDtypeStruct((latents, inner), BF16),
        in_specs=[whole()] * (len(latent) + 1),
        out_specs=pl.BlockSpec((block, inner), lambda i: (i, 0)),
        compiler_params=params(),
        cost_estimate=cost(2 * 1024 * inner * latents, 6 << 20),
        name="decoder_grad",
    )(*latent, res)


def exchange(rows):
    count, width = rows.shape
    return lax.all_to_all(
        rows.reshape(GROUPS, count // GROUPS, width), "feat", split_axis=0, concat_axis=0, tiled=True
    ).reshape(count, width)


def width_sum(part):
    for masks in ((1,), (4, 8, 12), (2,)):
        size = lax.axis_size("width")
        moved = [lax.ppermute(part, "width", [(a, a ^ m) for a in range(size)]) for m in masks]
        for other in moved:
            part = part + other
    return part


def per_device(acts, enc_weight, enc_bias, dec_weight, dec_bias, routes, latent_index):
    tokens, layers, width_dev = acts.shape
    inner = layers * width_dev
    latents = enc_weight.shape[3]
    scale = 1.0 / math.sqrt(L * D)
    x_home = in_vmem(acts.reshape(tokens, inner))
    enc = in_vmem(enc_weight.reshape(inner, latents))
    dec = in_vmem(dec_weight.reshape(latents, inner))
    bias = jnp.where(lax.axis_index("width") == 0, enc_bias, 0.0)

    info, *sends = pack(routes.T, x_home, latent_index.reshape(tokens, 2 * KEPT))
    arrived = [exchange(s) for s in sends]
    index, maps = slot_numbers(arrived[0])
    *later, token = slot_maps(index[1])
    maps.append(later)

    pre, latent, back, after, tokens_in = [], [], [], (), (token,)
    for c, cap in enumerate(CHUNKS):
        part = encode(in_vmem(arrived[c]), enc, bias, index[c], after)
        pre.append(width_sum(part))
        lat, decoded, token = decode(pre[c], *maps[c], dec, cap // PER, tokens_in)
        after, tokens_in = (token,), ()
        latent.append(lat)
        back.append(exchange(decoded))

    *turned, token = turn(arrived, inner)
    res = exchange(form_residual(info, x_home, dec_bias.reshape(1, inner), back, (token,)))
    lg = width_sum(latent_gradient(res, dec, index))
    grad_dec = decoder_grad(latent, res)
    grad_enc = encoder_grad(lg, pre, maps, turned, scale)
    return (
        grad_enc.reshape(1, layers, width_dev, latents),
        grad_dec.reshape(1, latents, layers, width_dev),
    )


def solution(mesh):
    placed = (
        P("feat", None, "width"),
        P("feat", None, "width", None),
        P("feat", None),
        P("feat", None, None, "width"),
        P(None, "width"),
        P("feat", None),
        P("feat", None, None),
    )
    return jax.shard_map(
        per_device,
        mesh=mesh,
        in_specs=placed,
        out_specs=(P("feat", None, "width", None), P("feat", None, None, "width")),
        check_vma=False,
    )
```

```python
import functools
import math

import jax
import jax.numpy as jnp
from jax import lax
from jax.experimental import pallas as pl
from jax.experimental.pallas import tpu as pltpu
from jax.sharding import PartitionSpec as P

D = 8192
L = 2
CAP = 64
GROUPS = 16
CHUNKS = (32, 32)
LANES = 128
BLOCK = 256
KEPT = 32
PER = LANES // KEPT
BF16 = jnp.bfloat16
F32 = jnp.float32
I32 = jnp.int32
VMEM_LIMIT = 20 * 1024 * 1024


def iota(shape, dim):
    return lax.broadcasted_iota(I32, shape, dim)


def params():
    return pltpu.CompilerParams(vmem_limit_bytes=VMEM_LIMIT)


def cost(flops, nbytes):
    return pl.CostEstimate(flops=int(flops), bytes_accessed=int(nbytes), transcendentals=0)


def hbm(shape, dtype):
    return pltpu.HBM(shape, dtype)


def vmem(shape, dtype):
    return pltpu.VMEM(shape, dtype)


def in_hbm(x):
    return pltpu.with_memory_space_constraint(x, pltpu.HBM)


def in_vmem(x):
    return pltpu.with_memory_space_constraint(x, pltpu.VMEM)


def whole():
    return pl.BlockSpec(memory_space=pltpu.VMEM)


def offsets():
    out, start = [], 0
    for cap in CHUNKS:
        out.append((start, cap))
        start += cap
    return out


def chunk_hits(info, off, cap, tokens):
    rows = iota((GROUPS * cap, tokens), 0)

    def slot(route, pos):
        inside = (pos >= off) & (pos < off + cap)
        return jnp.where(inside, route * cap + (pos - off), -1)

    return (rows == slot(info[0:1], info[1:2])) | (rows == slot(info[2:3], info[3:4]))


def pack_kernel(routes_ref, acts_ref, index_ref, info_ref, *send_refs):
    tokens, inner = acts_ref.shape
    upper = (iota((tokens, tokens), 0) < iota((tokens, tokens), 1)).astype(F32).astype(BF16)
    experts = iota((GROUPS, tokens), 0)
    total = jnp.zeros((GROUPS, 1), F32)
    rows = []
    for j in range(2):
        route = routes_ref[j : j + 1, :]
        hit = experts == route
        hot = hit.astype(F32)
        before = jnp.dot(hot.astype(BF16), upper, preferred_element_type=F32) + total
        total = total + jnp.sum(hot, axis=1, keepdims=True)
        pos = jnp.sum(jnp.where(hit, before, 0.0), axis=0, keepdims=True).astype(I32)
        rows += [route, pos]
    info = jnp.concatenate(rows + [jnp.zeros((4, tokens), I32)], axis=0)
    info_ref[...] = info
    x = acts_ref[...]
    for (off, cap), send_ref in zip(offsets(), send_refs):
        hits = chunk_hits(info, off, cap, tokens).astype(F32).astype(BF16)
        send_ref[:, :inner] = jnp.dot(hits, x, preferred_element_type=F32).astype(BF16)
    send_refs[0][:, inner:] = index_codes(info, index_ref[...])


def index_codes(info, index):
    tokens, cols = index.shape
    code = (((index & 127) + 128) << (index >> 7)).astype(F32).astype(BF16)
    col = iota((cols, LANES), 0)
    lane = iota((cols, LANES), 1)
    first = CHUNKS[0]
    rows_total = GROUPS * first
    row = iota((rows_total, tokens), 0)
    expert, inner = row // first, row % first
    base = jnp.full((rows_total, tokens), -(1 << 20), I32)
    step = jnp.zeros((rows_total, tokens), I32)
    for off, cap in offsets():
        here = (inner >= off // PER) & (inner < (off + cap) // PER)
        base = jnp.where(here, expert * CAP + off + inner - off // PER, base)
        step = jnp.where(here, cap // PER, step)
    lane_q = iota((rows_total, LANES), 1) // KEPT
    result = jnp.zeros((rows_total, LANES), F32)
    for j in range(2):
        spread = (col == j * KEPT + lane % KEPT).astype(F32).astype(BF16)
        codes = jnp.dot(code, spread, preferred_element_type=F32).astype(BF16)
        key = info[2 * j : 2 * j + 1] * CAP + info[2 * j + 1 : 2 * j + 2]
        for q in range(PER):
            hit = (base + step * q == key).astype(F32).astype(BF16)
            picked = jnp.dot(hit, codes, preferred_element_type=F32)
            result = result + jnp.where(lane_q == q, picked, 0.0)
    return result.astype(BF16)


def pack(routes_t, x, index):
    tokens, width = x.shape
    widths = [width + LANES] + [width] * (len(CHUNKS) - 1)
    return pl.pallas_call(
        pack_kernel,
        out_shape=(jax.ShapeDtypeStruct((8, tokens), I32),)
        + tuple(jax.ShapeDtypeStruct((GROUPS * c, w), BF16) for c, w in zip(CHUNKS, widths)),
        in_specs=[whole()] * 3,
        out_specs=(whole(),) * (1 + len(CHUNKS)),
        compiler_params=params(),
        cost_estimate=cost(2 * GROUPS * CAP * tokens * width, 3 << 20),
        name="pack_tokens",
    )(routes_t, x, index)


def numbers_kernel(codes_ref, *refs):
    first = CHUNKS[0]
    code = codes_ref[...].astype(F32).astype(I32)
    tile = jnp.zeros(code.shape, I32)
    for h in range(7):
        tile = tile + jnp.where(code >= (256 << h), 1, 0)
    numbers = jnp.where(code > 0, tile * 128 + (code >> tile) - 128, -1)
    for (off, cap), index_ref in zip(offsets(), refs):
        for src in range(GROUPS):
            start = src * first + off // PER
            index_ref[src] = numbers[start : start + cap // PER]
    maps_kernel(refs[0], *refs[len(CHUNKS) :])


def maps_kernel(index_ref, low_ref, high_ref, scratch_ref):
    packed = index_ref.shape[1]
    cap = packed * PER
    turned = jnp.concatenate([index_ref[src] for src in range(GROUPS)], axis=0).T
    tile = turned >> 7
    scratch_ref[0] = jnp.where(turned >= 0, turned & 127, -1)
    place = (iota(turned.shape, 0) % KEPT) + 1
    scratch_ref[1] = jnp.where((tile >= 0) & (tile < 4), place << (jnp.clip(tile, 0, 3) * 6), 0)
    scratch_ref[2] = jnp.where(tile >= 4, place << (jnp.clip(tile - 4, 0, 3) * 6), 0)
    for q in range(PER):
        lows, highs = [], []
        for part in range(2):
            size = LANES // 2
            spot = iota((size, LANES), 0) + part * size
            low = jnp.zeros((size, LANES), I32)
            high = jnp.zeros((size, LANES), I32)
            for k in range(KEPT):
                at = q * KEPT + k
                same = spot == scratch_ref[0, at : at + 1, :]
                low = low + jnp.where(same, scratch_ref[1, at : at + 1, :], 0)
                high = high + jnp.where(same, scratch_ref[2, at : at + 1, :], 0)
            lows.append(low)
            highs.append(high)
        low = jnp.concatenate(lows, axis=0).T
        high = jnp.concatenate(highs, axis=0).T
        for src in range(GROUPS):
            row = src * cap + q * packed
            low_ref[row : row + packed, :] = low[src * packed : (src + 1) * packed]
            high_ref[row : row + packed, :] = high[src * packed : (src + 1) * packed]


def map_shapes(cap):
    return [jax.ShapeDtypeStruct((GROUPS * cap, LANES), I32)] * 2


def slot_numbers(arrived):
    rows, width = arrived.shape
    shapes = [jax.ShapeDtypeStruct((GROUPS, cap // PER, LANES), I32) for cap in CHUNKS]
    shapes += map_shapes(CHUNKS[0])
    out = pl.pallas_call(
        numbers_kernel,
        grid=(1,),
        out_shape=tuple(shapes),
        in_specs=[pl.BlockSpec((rows, LANES), lambda i: (0, width // LANES - 1))],
        out_specs=tuple(
            pl.BlockSpec(s.shape, functools.partial(lambda n, i: (0,) * n, len(s.shape))) for s in shapes
        ),
        scratch_shapes=[pltpu.VMEM((3, LANES, LANES), I32)],
        compiler_params=params(),
        cost_estimate=cost(2_000_000_000, 1 << 20),
        name="slot_numbers",
    )(arrived)
    return out[: len(CHUNKS)], [out[len(CHUNKS) :]]


def later_maps_kernel(index_ref, low_ref, high_ref, token_ref, scratch_ref):
    token_ref[...] = jnp.zeros_like(token_ref)
    maps_kernel(index_ref, low_ref, high_ref, scratch_ref)


def slot_maps(index):
    cap = index.shape[1] * PER
    return pl.pallas_call(
        later_maps_kernel,
        out_shape=tuple(map_shapes(cap)) + (TOKEN,),
        in_specs=[whole()],
        out_specs=(whole(),) * 3,
        scratch_shapes=[pltpu.VMEM((3, LANES, LANES), I32)],
        compiler_params=params(),
        cost_estimate=cost(2_000_000_000, 1 << 20),
        name="slot_maps",
    )(index)


def skipping(kernel, inputs, extra):
    def run(*refs):
        kernel(*refs[:inputs], *refs[inputs + extra :])

    return run


TOKEN = jax.ShapeDtypeStruct((8, LANES), F32)


def token_spec():
    return pl.BlockSpec((8, LANES), lambda *i: (0, 0))


def gather_kept(values_ref, index_ref, out_ref, stride, base, start):
    tiles = values_ref.shape[1] // LANES
    packed_rows = index_ref.shape[1]
    lane_q = iota((8, LANES), 1) // KEPT
    for src in range(GROUPS):
        for half in range(packed_rows // 8):
            idx = index_ref[src, half * 8 : half * 8 + 8, :]
            spot, tile = idx & 127, idx >> 7
            result = jnp.zeros((8, LANES), F32)
            for q in range(PER):
                row = src * stride + base + q * packed_rows + half * 8
                here = jnp.where(lane_q == q, tile, -1)
                for t in range(tiles):
                    part = values_ref[row : row + 8, t * LANES : (t + 1) * LANES]
                    taken = jnp.take_along_axis(part, spot, axis=1, mode="promise_in_bounds")
                    result = jnp.where(here == t, taken, result)
            place = start + src * packed_rows + half * 8
            out_ref[place : place + 8, :] = result


def encode_kernel(x_ref, w_ref, bias_ref, index_ref, out_ref, values_ref):
    inner = w_ref.shape[0]
    values_ref[...] = (
        jnp.dot(x_ref[:, :inner], w_ref[...], preferred_element_type=F32) + bias_ref[...]
    )
    gather_kept(values_ref, index_ref, out_ref, index_ref.shape[1] * PER, 0, 0)


def encode(rows, weight, bias, index, after):
    total, latents = rows.shape[0], weight.shape[1]
    return pl.pallas_call(
        skipping(encode_kernel, 4, len(after)),
        out_shape=jax.ShapeDtypeStruct((total // PER, LANES), F32),
        in_specs=[whole()] * (4 + len(after)),
        out_specs=whole(),
        scratch_shapes=[pltpu.VMEM((total, latents), F32)],
        compiler_params=params(),
        cost_estimate=cost(4 * total * 1024 * latents, 4 << 20),
        name="encode",
    )(rows, weight, bias, index, *after)


def encode_streamed_kernel(x_ref, w_ref, bias_ref, index_ref, out_ref, values_ref, x_held, w_held, sem_ref):
    inner, latents = w_ref.shape
    steps = inner // BLOCK
    reads = []
    for k in range(steps):
        here = pl.ds(k * BLOCK, BLOCK)
        reads.append(
            (
                pltpu.make_async_copy(x_ref.at[:, here], x_held.at[:, here], sem_ref.at[0, k]),
                pltpu.make_async_copy(w_ref.at[here, :], w_held.at[here, :], sem_ref.at[1, k]),
            )
        )
        for copy in reads[-1]:
            copy.start()
    for k in range(steps):
        for copy in reads[k]:
            copy.wait()
        here = pl.ds(k * BLOCK, BLOCK)
        part = jnp.dot(x_held[:, here], w_held[here, :], preferred_element_type=F32)
        if k == 0:
            values_ref[...] = part + bias_ref[...]
        else:
            values_ref[...] += part
    gather_kept(values_ref, index_ref, out_ref, index_ref.shape[1] * PER, 0, 0)


def encode_streamed(rows, weight, bias, index, after):
    total, (inner, latents) = rows.shape[0], weight.shape
    return pl.pallas_call(
        skipping(encode_streamed_kernel, 4, len(after)),
        out_shape=jax.ShapeDtypeStruct((total // PER, LANES), F32),
        in_specs=[pl.BlockSpec(memory_space=pl.ANY)] * 2 + [whole()] * (2 + len(after)),
        out_specs=whole(),
        scratch_shapes=[
            pltpu.VMEM((total, latents), F32),
            pltpu.VMEM((total, inner), BF16),
            pltpu.VMEM((inner, latents), BF16),
            pltpu.SemaphoreType.DMA((2, inner // BLOCK)),
        ],
        compiler_params=params(),
        cost_estimate=cost(4 * total * inner * latents, 4 << 20),
        name="encode_streamed",
    )(in_hbm(rows), in_hbm(weight), bias, index, *after)


def latent_gradient_kernel(r_ref, w_ref, *refs):
    index_refs, out_ref, values_ref = refs[:-2], refs[-2], refs[-1]
    values_ref[...] = lax.dot_general(
        r_ref[...], w_ref[...], (((1,), (1,)), ((), ())), preferred_element_type=F32
    )
    start = 0
    for (off, cap), index_ref in zip(offsets(), index_refs):
        gather_kept(values_ref, index_ref, out_ref, CAP, off, start)
        start += GROUPS * cap // PER


def latent_gradient(rows, weight, index):
    total, latents = rows.shape[0], weight.shape[0]
    return pl.pallas_call(
        latent_gradient_kernel,
        out_shape=jax.ShapeDtypeStruct((total // PER, LANES), F32),
        in_specs=[whole()] * (2 + len(index)),
        out_specs=whole(),
        scratch_shapes=[pltpu.VMEM((total, latents), F32)],
        compiler_params=params(),
        cost_estimate=cost(4 * total * 1024 * latents, 4 << 20),
        name="latent_gradient",
    )(rows, weight, *index)


def spread_kept(kept_ref, low_ref, high_ref, dense_ref, packed_rows, tiles, source=0, target=0):
    for src in range(GROUPS):
        place = source + src * packed_rows
        kept = kept_ref[place : place + packed_rows, :]
        for q in range(0, PER, 2):
            row = src * packed_rows * PER + q * packed_rows
            for column, t in enumerate(tiles):
                word_ref = (low_ref, high_ref)[t // 4]
                pieces = []
                for half in range(2):
                    start = row + half * packed_rows
                    which = (word_ref[start : start + packed_rows, :] >> (6 * (t % 4))) & 63
                    spot = jnp.maximum(which - 1, 0) + (q + half) * KEPT
                    taken = jnp.take_along_axis(kept, spot, axis=1, mode="promise_in_bounds")
                    pieces.append(jnp.where(which > 0, taken, 0.0))
                rows = slice(target + row, target + row + 2 * packed_rows)
                dense_ref[rows, column * LANES : (column + 1) * LANES] = jnp.concatenate(
                    pieces, axis=0
                ).astype(BF16)


def spread_latents(pre_ref, low_ref, high_ref, kept_ref, rows_ref):
    pre = pre_ref[...]
    kept_ref[...] = (pre / (1.0 + jnp.exp(-pre))).astype(BF16).astype(F32)
    tiles = range(rows_ref.shape[1] // LANES)
    spread_kept(kept_ref, low_ref, high_ref, rows_ref, pre_ref.shape[0] // GROUPS, tiles)


def decode_kernel(pre_ref, low_ref, high_ref, w_ref, out_ref, token_ref, kept_ref, rows_ref, made_ref, sem_ref):
    token_ref[...] = jnp.zeros_like(token_ref)
    spread_latents(pre_ref, low_ref, high_ref, kept_ref, rows_ref)
    copies = []
    for j in range(w_ref.shape[1] // BLOCK):
        here = pl.ds(j * BLOCK, BLOCK)
        made_ref[:, here] = jnp.dot(
            rows_ref[...], w_ref[:, here], preferred_element_type=F32
        ).astype(BF16)
        copy = pltpu.make_async_copy(made_ref.at[:, here], out_ref.at[:, here], sem_ref.at[j])
        copy.start()
        copies.append(copy)
    for copy in copies:
        copy.wait()


def anywhere():
    return pl.BlockSpec(memory_space=pl.ANY)


def decode(pre, low, high, weight, after):
    total = low.shape[0]
    latents, inner = weight.shape
    return pl.pallas_call(
        skipping(decode_kernel, 4, len(after)),
        out_shape=(hbm((total, inner), BF16), TOKEN),
        in_specs=[whole()] * (4 + len(after)),
        out_specs=(anywhere(), whole()),
        scratch_shapes=[
            pltpu.VMEM(pre.shape, F32),
            pltpu.VMEM((total, latents), BF16),
            pltpu.VMEM((total, inner), BF16),
            pltpu.SemaphoreType.DMA((inner // BLOCK,)),
        ],
        compiler_params=params(),
        cost_estimate=cost(4 * total * inner * latents, 6 << 20),
        name="decode",
    )(pre, low, high, weight, *after)


def latents_kernel(*refs):
    count = len(CHUNKS)
    pre_refs, map_refs = refs[:count], refs[count : 3 * count]
    out_refs, token_ref, rows_refs = refs[3 * count : 4 * count], refs[4 * count], refs[4 * count + 1 : 5 * count + 1]
    kept_refs, sem_ref = refs[5 * count + 1 : -1], refs[-1]
    token_ref[...] = jnp.zeros_like(token_ref)
    copies = []
    for c in range(count):
        spread_latents(pre_refs[c], *map_refs[2 * c : 2 * c + 2], kept_refs[c], rows_refs[c])
        copies.append(pltpu.make_async_copy(rows_refs[c], out_refs[c], sem_ref.at[c]))
        copies[-1].start()
    for copy in copies:
        copy.wait()


def make_latents(pre, maps, latents):
    rows = [p.shape[0] * PER for p in pre]
    *out, token = pl.pallas_call(
        latents_kernel,
        out_shape=tuple(hbm((n, latents), BF16) for n in rows) + (TOKEN,),
        in_specs=[whole()] * (3 * len(pre)),
        out_specs=(anywhere(),) * len(pre) + (whole(),),
        scratch_shapes=[pltpu.VMEM((n, latents), BF16) for n in rows]
        + [pltpu.VMEM(p.shape, F32) for p in pre]
        + [pltpu.SemaphoreType.DMA((len(pre),))],
        compiler_params=params(),
        cost_estimate=cost(4_000_000_000, 4 << 20),
        name="make_latents",
    )(*pre, *[m for pair in maps for m in pair])
    return out, token


def residual_kernel(*refs):
    count = len(CHUNKS)
    info_ref, x_ref, bias_ref = refs[:3]
    back_refs, send_ref = refs[3 : 3 + count], refs[3 + count]
    tokens = x_ref.shape[0]
    info = info_ref[...]
    total = jnp.zeros(x_ref.shape, F32)
    for (off, cap), back_ref in zip(offsets(), back_refs):
        hit = chunk_hits(info, off, cap, tokens).astype(F32).astype(BF16)
        total = total + lax.dot_general(
            hit, back_ref[...], (((0,), (0,)), ((), ())), preferred_element_type=F32
        )
    residual = (total + bias_ref[...] - x_ref[...].astype(F32)).astype(BF16)
    hit = chunk_hits(info, 0, CAP, tokens).astype(F32).astype(BF16)
    send_ref[...] = jnp.dot(hit, residual, preferred_element_type=F32).astype(BF16)


def form_residual(info, x, bias, back, after):
    tokens, width = x.shape
    return pl.pallas_call(
        skipping(residual_kernel, 3 + len(CHUNKS), len(after)),
        out_shape=jax.ShapeDtypeStruct((GROUPS * CAP, width), BF16),
        in_specs=[whole()] * (3 + len(CHUNKS) + len(after)),
        out_specs=whole(),
        compiler_params=params(),
        cost_estimate=cost(4 * GROUPS * CAP * tokens * width, 5 << 20),
        name="form_residual",
    )(info, x, bias, *back, *after)


def turn_kernel(*refs):
    half = (len(refs) - 1) // 2
    refs[-1][...] = jnp.zeros(refs[-1].shape, F32)
    for src, dst in zip(refs[:half], refs[half:]):
        block = dst.shape[0]
        here = pl.ds(pl.multiple_of(pl.program_id(0) * block, block), block)
        dst[...] = src[:, here].T


def turn(arrived, inner):
    return pl.pallas_call(
        turn_kernel,
        grid=(4,),
        out_shape=tuple(hbm((inner, a.shape[0]), BF16) for a in arrived) + (TOKEN,),
        in_specs=[whole()] * len(arrived),
        out_specs=tuple(pl.BlockSpec((inner // 4, a.shape[0]), lambda i: (i, 0)) for a in arrived)
        + (token_spec(),),
        compiler_params=params(),
        cost_estimate=cost(4_000_000_000, 4 << 20),
        name="turn_rows",
    )(*arrived)


def encoder_grad_kernel(scale, lg_ref, *refs):
    count = len(CHUNKS)
    pre_refs, map_refs, x_refs = refs[:count], refs[count : 3 * count], refs[3 * count : 4 * count]
    out_ref, kept_ref, grad_ref, made_ref = refs[4 * count : 4 * count + 4]
    held_refs, read_sem, sem_ref = refs[4 * count + 4 : -2], refs[-2], refs[-1]
    reads = [
        pltpu.make_async_copy(x_ref, held_ref, read_sem.at[c])
        for c, (x_ref, held_ref) in enumerate(zip(x_refs, held_refs))
    ]
    for copy in reads:
        copy.start()
    starts, start = [], 0
    for c, cap in enumerate(CHUNKS):
        packed = GROUPS * cap // PER
        pre = pre_refs[c][...]
        sig = 1.0 / (1.0 + jnp.exp(-pre))
        slope = lg_ref[start : start + packed, :] * (sig * (1.0 + pre * (1.0 - sig)))
        kept_ref[start : start + packed, :] = slope.astype(BF16).astype(F32)
        starts.append(start)
        start += packed

    def spread(j):
        for c, cap in enumerate(CHUNKS):
            tiles = range(j * BLOCK // LANES, (j + 1) * BLOCK // LANES)
            words = map_refs[2 * c : 2 * c + 2]
            spread_kept(
                kept_ref, *words, grad_ref.at[j], cap // PER, tiles, starts[c], starts[c] * PER
            )

    blocks = grad_ref.shape[0]
    spread(0)
    for copy in reads:
        copy.wait()
    writes = []
    for j in range(blocks):
        if j + 1 < blocks:
            spread(j + 1)
        total = None
        for c, cap in enumerate(CHUNKS):
            rows = slice(starts[c] * PER, starts[c] * PER + GROUPS * cap)
            part = jnp.dot(held_refs[c][...], grad_ref[j, rows, :], preferred_element_type=F32)
            total = part if total is None else total + part
        made_ref[j] = (total * scale).astype(BF16)
        copy = pltpu.make_async_copy(
            made_ref.at[j], out_ref.at[:, pl.ds(j * BLOCK, BLOCK)], sem_ref.at[j]
        )
        copy.start()
        writes.append(copy)
    for copy in writes:
        copy.wait()


def encoder_grad(lg, pre, maps, turned, scale):
    latents = 1024
    inner = turned[0].shape[0]
    blocks = latents // BLOCK
    operands = [lg, *pre, *[m for pair in maps for m in pair]]
    return pl.pallas_call(
        functools.partial(encoder_grad_kernel, scale),
        out_shape=jax.ShapeDtypeStruct((inner, latents), BF16),
        in_specs=[whole()] * len(operands) + [anywhere()] * len(turned),
        out_specs=anywhere(),
        scratch_shapes=[
            pltpu.VMEM(lg.shape, F32),
            pltpu.VMEM((blocks, GROUPS * CAP, BLOCK), BF16),
            pltpu.VMEM((blocks, inner, BLOCK), BF16),
        ]
        + [pltpu.VMEM(t.shape, BF16) for t in turned]
        + [pltpu.SemaphoreType.DMA((len(turned),)), pltpu.SemaphoreType.DMA((blocks,))],
        compiler_params=params(),
        cost_estimate=cost(4 * 1024 * inner * latents, 6 << 20),
        name="encoder_grad",
    )(*operands, *[in_hbm(t) for t in turned])


def decoder_grad_kernel(*refs):
    latent_refs, res_ref, out_ref, token_ref = refs[:-3], refs[-3], refs[-2], refs[-1]
    token_ref[...] = jnp.zeros_like(token_ref)
    block = out_ref.shape[0]
    here = pl.ds(pl.multiple_of(pl.program_id(0) * block, block), block)
    total = None
    for (off, cap), latent_ref in zip(offsets(), latent_refs):
        rows = [res_ref[src * CAP + off : src * CAP + off + cap, :] for src in range(GROUPS)]
        part = lax.dot_general(
            latent_ref[:, here],
            jnp.concatenate(rows, axis=0),
            (((0,), (0,)), ((), ())),
            preferred_element_type=F32,
        )
        total = part if total is None else total + part
    out_ref[...] = total.astype(BF16)


def decoder_grad(latent, res):
    latents, inner = latent[0].shape[1], res.shape[1]
    block = 256
    return pl.pallas_call(
        decoder_grad_kernel,
        grid=(latents // block,),
        out_shape=(jax.ShapeDtypeStruct((latents, inner), BF16), TOKEN),
        in_specs=[whole()] * (len(latent) + 1),
        out_specs=(pl.BlockSpec((block, inner), lambda i: (i, 0)), token_spec()),
        compiler_params=params(),
        cost_estimate=cost(2 * 1024 * inner * latents, 6 << 20),
        name="decoder_grad",
    )(*latent, res)


def exchange(rows):
    count, width = rows.shape
    return lax.all_to_all(
        rows.reshape(GROUPS, count // GROUPS, width), "feat", split_axis=0, concat_axis=0, tiled=True
    ).reshape(count, width)


def add_kernel(*refs):
    total = refs[0][...]
    for ref in refs[1:-1]:
        total = total + ref[...]
    refs[-1][...] = total


def add_after(parts, after):
    return pl.pallas_call(
        skipping(add_kernel, len(parts), 1),
        out_shape=jax.ShapeDtypeStruct(parts[0].shape, F32),
        in_specs=[whole()] * (len(parts) + 1),
        out_specs=whole(),
        compiler_params=params(),
        name="add_parts",
    )(*parts, after)


def width_sum(part, between=None):
    for masks in ((1,), (4, 8, 12), (2,)):
        size = lax.axis_size("width")
        moved = [lax.ppermute(part, "width", [(a, a ^ m) for a in range(size)]) for m in masks]
        if between is not None and len(masks) > 1:
            part = add_after([part, *moved], between)
            continue
        for other in moved:
            part = part + other
    return part


def per_device(acts, enc_weight, enc_bias, dec_weight, dec_bias, routes, latent_index):
    tokens, layers, width_dev = acts.shape
    inner = layers * width_dev
    latents = enc_weight.shape[3]
    scale = 1.0 / math.sqrt(L * D)
    x_home = in_vmem(acts.reshape(tokens, inner))
    enc = enc_weight.reshape(inner, latents)
    dec = in_vmem(dec_weight.reshape(latents, inner))
    bias = jnp.where(lax.axis_index("width") == 0, enc_bias, 0.0)

    info, *sends = pack(routes.T, x_home, latent_index.reshape(tokens, 2 * KEPT))
    arrived = [exchange(s) for s in sends]
    index, maps = slot_numbers(arrived[0])
    *later, token = slot_maps(index[1])
    maps.append(later)

    pre, back, after, tokens_in = [], [], (), (token,)
    for c in range(len(CHUNKS)):
        if c == 0:
            part = encode(arrived[c], in_vmem(enc), bias, index[c], after)
        else:
            part = encode_streamed(arrived[c], enc, bias, index[c], after)
        pre.append(width_sum(part))
        decoded, token = decode(pre[c], *maps[c], dec, tokens_in)
        after, tokens_in = (token,), ()
        back.append(exchange(decoded))

    *turned, token = turn(arrived, inner)
    latent, later = make_latents(pre, maps, latents)
    res = exchange(form_residual(info, x_home, dec_bias.reshape(1, inner), back, (token, later)))
    grad_dec, token = decoder_grad(latent, res)
    lg = width_sum(latent_gradient(res, dec, index), token)
    grad_enc = encoder_grad(lg, pre, maps, turned, scale)
    return (
        grad_enc.reshape(1, layers, width_dev, latents),
        grad_dec.reshape(1, latents, layers, width_dev),
    )


def solution(mesh):
    placed = (
        P("feat", None, "width"),
        P("feat", None, "width", None),
        P("feat", None),
        P("feat", None, None, "width"),
        P(None, "width"),
        P("feat", None),
        P("feat", None, None),
    )
    return jax.shard_map(
        per_device,
        mesh=mesh,
        in_specs=placed,
        out_specs=(P("feat", None, "width", None), P("feat", None, None, "width")),
        check_vma=False,
    )
```

```python
import functools
import math

import jax
import jax.numpy as jnp
from jax import lax
from jax.experimental import pallas as pl
from jax.experimental.pallas import tpu as pltpu
from jax.sharding import PartitionSpec as P

D = 8192
L = 2
CAP = 64
GROUPS = 16
CHUNKS = (32, 32)
LANES = 128
BLOCK = 256
KEPT = 32
PER = LANES // KEPT
BF16 = jnp.bfloat16
F32 = jnp.float32
I32 = jnp.int32
VMEM_LIMIT = 20 * 1024 * 1024


def iota(shape, dim):
    return lax.broadcasted_iota(I32, shape, dim)


def params():
    return pltpu.CompilerParams(vmem_limit_bytes=VMEM_LIMIT)


def cost(flops, nbytes):
    return pl.CostEstimate(flops=int(flops), bytes_accessed=int(nbytes), transcendentals=0)


def hbm(shape, dtype):
    return pltpu.HBM(shape, dtype)


def vmem(shape, dtype):
    return pltpu.VMEM(shape, dtype)


def in_hbm(x):
    return pltpu.with_memory_space_constraint(x, pltpu.HBM)


def in_vmem(x):
    return pltpu.with_memory_space_constraint(x, pltpu.VMEM)


def whole():
    return pl.BlockSpec(memory_space=pltpu.VMEM)


PLACES = CHUNKS[0] // PER
PACKED = GROUPS * PLACES


def quarter_keys(tokens):
    row = iota((PACKED, tokens), 0)
    return (row // PLACES) * CAP + row % PLACES


def token_keys(info):
    return [info[2 * j : 2 * j + 1] * CAP + info[2 * j + 1 : 2 * j + 2] for j in range(2)]


def as_ones(hit):
    return hit.astype(F32).astype(BF16)


def quarters(x, width=1024):
    return jnp.concatenate([x[:, i * width : (i + 1) * width] for i in range(x.shape[1] // width)], axis=0)


def pack_kernel(routes_ref, acts_ref, index_ref, info_ref, *send_refs):
    tokens, inner = acts_ref.shape
    upper = as_ones(iota((tokens, tokens), 0) < iota((tokens, tokens), 1))
    experts = iota((GROUPS, tokens), 0)
    total = jnp.zeros((GROUPS, 1), F32)
    rows = []
    for j in range(2):
        route = routes_ref[j : j + 1, :]
        hit = experts == route
        hot = hit.astype(F32)
        before = jnp.dot(hot.astype(BF16), upper, preferred_element_type=F32) + total
        total = total + jnp.sum(hot, axis=1, keepdims=True)
        pos = jnp.sum(jnp.where(hit, before, 0.0), axis=0, keepdims=True).astype(I32)
        rows += [route, pos]
    info = jnp.concatenate(rows + [jnp.zeros((4, tokens), I32)], axis=0)
    info_ref[...] = info
    x = acts_ref[...]
    index = index_ref[...]
    code = (((index & 127) + 128) << (index >> 7)).astype(F32).astype(BF16)
    cols = index.shape[1]
    col = iota((cols, LANES), 0)
    lane = iota((cols, LANES), 1)
    codes = [
        jnp.dot(code, as_ones(col == j * KEPT + lane % KEPT), preferred_element_type=F32).astype(BF16)
        for j in range(2)
    ]
    first = quarter_keys(tokens)
    keys = token_keys(info)
    lane_q = iota((PACKED, LANES), 1) // KEPT
    for c, send_ref in enumerate(send_refs):
        kept = jnp.zeros((PACKED, LANES), F32)
        for q in range(PER):
            slot = first + (c * PER + q) * PLACES
            hits = [slot == key for key in keys]
            send_ref[:, q * inner : (q + 1) * inner] = jnp.dot(
                as_ones(hits[0] | hits[1]), x, preferred_element_type=F32
            ).astype(BF16)
            for hit, route_codes in zip(hits, codes):
                picked = jnp.dot(as_ones(hit), route_codes, preferred_element_type=F32)
                kept = kept + jnp.where(lane_q == q, picked, 0.0)
        send_ref[:, PER * inner :] = kept.astype(BF16)


def pack(routes_t, x, index):
    tokens, width = x.shape
    send = jax.ShapeDtypeStruct((PACKED, PER * width + LANES), BF16)
    return pl.pallas_call(
        pack_kernel,
        out_shape=(jax.ShapeDtypeStruct((8, tokens), I32),) + (send,) * len(CHUNKS),
        in_specs=[whole()] * 3,
        out_specs=(whole(),) * (1 + len(CHUNKS)),
        compiler_params=params(),
        cost_estimate=cost(2 * GROUPS * CAP * tokens * width, 3 << 20),
        name="pack_tokens",
    )(routes_t, x, index)


def maps_kernel(codes_ref, index_ref, low_ref, high_ref, scratch_ref):
    code = codes_ref[...].astype(F32).astype(I32)
    tile = jnp.zeros(code.shape, I32)
    for h in range(7):
        tile = tile + jnp.where(code >= (256 << h), 1, 0)
    numbers = jnp.where(code > 0, tile * 128 + (code >> tile) - 128, -1)
    index_ref[...] = numbers
    turned = numbers.T
    tile = turned >> 7
    scratch_ref[0] = jnp.where(turned >= 0, turned & 127, -1)
    place = (iota(turned.shape, 0) % KEPT) + 1
    scratch_ref[1] = jnp.where((tile >= 0) & (tile < 4), place << (jnp.clip(tile, 0, 3) * 6), 0)
    scratch_ref[2] = jnp.where(tile >= 4, place << (jnp.clip(tile - 4, 0, 3) * 6), 0)
    for q in range(PER):
        lows, highs = [], []
        for part in range(2):
            size = LANES // 2
            spot = iota((size, LANES), 0) + part * size
            low = jnp.zeros((size, LANES), I32)
            high = jnp.zeros((size, LANES), I32)
            for k in range(KEPT):
                at = q * KEPT + k
                same = spot == scratch_ref[0, at : at + 1, :]
                low = low + jnp.where(same, scratch_ref[1, at : at + 1, :], 0)
                high = high + jnp.where(same, scratch_ref[2, at : at + 1, :], 0)
            lows.append(low)
            highs.append(high)
        rows = slice(q * PACKED, (q + 1) * PACKED)
        low_ref[rows, :] = jnp.concatenate(lows, axis=0).T
        high_ref[rows, :] = jnp.concatenate(highs, axis=0).T


def slot_maps(arrived):
    rows, width = arrived.shape
    shapes = [jax.ShapeDtypeStruct((PACKED, LANES), I32)]
    shapes += [jax.ShapeDtypeStruct((PER * PACKED, LANES), I32)] * 2
    index, low, high = pl.pallas_call(
        maps_kernel,
        grid=(1,),
        out_shape=tuple(shapes),
        in_specs=[pl.BlockSpec((rows, LANES), lambda i: (0, width // LANES - 1))],
        out_specs=tuple(pl.BlockSpec(s.shape, lambda i: (0, 0)) for s in shapes),
        scratch_shapes=[pltpu.VMEM((3, LANES, LANES), I32)],
        compiler_params=params(),
        cost_estimate=cost(2_000_000_000, 1 << 20),
        name="slot_maps",
    )(arrived)
    return index, (low, high)


def skipping(kernel, inputs, extra):
    def run(*refs):
        kernel(*refs[:inputs], *refs[inputs + extra :])

    return run


TOKEN = jax.ShapeDtypeStruct((8, LANES), F32)


def token_spec():
    return pl.BlockSpec((8, LANES), lambda *i: (0, 0))


def gather_kept(values_ref, index_ref, out_ref, base, start):
    tiles = values_ref.shape[1] // LANES
    lane_q = iota((8, LANES), 1) // KEPT
    for group in range(0, PACKED, 8):
        idx = index_ref[group : group + 8, :]
        spot, tile = idx & 127, idx >> 7
        result = jnp.zeros((8, LANES), F32)
        for q in range(PER):
            row = base + q * PACKED + group
            here = jnp.where(lane_q == q, tile, -1)
            for t in range(tiles):
                part = values_ref[row : row + 8, t * LANES : (t + 1) * LANES]
                taken = jnp.take_along_axis(part, spot, axis=1, mode="promise_in_bounds")
                result = jnp.where(here == t, taken, result)
        out_ref[start + group : start + group + 8, :] = result


def encode_kernel(x_ref, w_ref, bias_ref, index_ref, out_ref, values_ref):
    x = quarters(x_ref[:, : PER * w_ref.shape[0]])
    values_ref[...] = jnp.dot(x, w_ref[...], preferred_element_type=F32) + bias_ref[...]
    gather_kept(values_ref, index_ref, out_ref, 0, 0)


def encode(rows, weight, bias, index, after):
    inner, latents = weight.shape
    return pl.pallas_call(
        skipping(encode_kernel, 4, len(after)),
        out_shape=jax.ShapeDtypeStruct((PACKED, LANES), F32),
        in_specs=[whole()] * (4 + len(after)),
        out_specs=whole(),
        scratch_shapes=[pltpu.VMEM((PER * PACKED, latents), F32)],
        compiler_params=params(),
        cost_estimate=cost(4 * PER * PACKED * inner * latents, 4 << 20),
        name="encode",
    )(rows, weight, bias, index, *after)


def encode_streamed_kernel(x_ref, w_ref, bias_ref, index_ref, out_ref, values_ref, x_held, w_held, sem_ref):
    inner, latents = w_ref.shape
    steps = inner // BLOCK
    reads = []
    for k in range(steps):
        here = pl.ds(k * BLOCK, BLOCK)
        reads.append([pltpu.make_async_copy(w_ref.at[here, :], w_held.at[here, :], sem_ref.at[PER, k])])
        for q in range(PER):
            source = x_ref.at[:, pl.ds(q * inner + k * BLOCK, BLOCK)]
            target = x_held.at[pl.ds(q * PACKED, PACKED), here]
            reads[-1].append(pltpu.make_async_copy(source, target, sem_ref.at[q, k]))
        for copy in reads[-1]:
            copy.start()
    for k in range(steps):
        for copy in reads[k]:
            copy.wait()
        here = pl.ds(k * BLOCK, BLOCK)
        part = jnp.dot(x_held[:, here], w_held[here, :], preferred_element_type=F32)
        if k == 0:
            values_ref[...] = part + bias_ref[...]
        else:
            values_ref[...] += part
    gather_kept(values_ref, index_ref, out_ref, 0, 0)


def encode_streamed(rows, weight, bias, index, after):
    total, (inner, latents) = PER * PACKED, weight.shape
    return pl.pallas_call(
        skipping(encode_streamed_kernel, 4, len(after)),
        out_shape=jax.ShapeDtypeStruct((PACKED, LANES), F32),
        in_specs=[pl.BlockSpec(memory_space=pl.ANY)] * 2 + [whole()] * (2 + len(after)),
        out_specs=whole(),
        scratch_shapes=[
            pltpu.VMEM((total, latents), F32),
            pltpu.VMEM((total, inner), BF16),
            pltpu.VMEM((inner, latents), BF16),
            pltpu.SemaphoreType.DMA((PER + 1, inner // BLOCK)),
        ],
        compiler_params=params(),
        cost_estimate=cost(4 * total * inner * latents, 4 << 20),
        name="encode_streamed",
    )(in_hbm(rows), in_hbm(weight), bias, index, *after)


def latent_gradient_kernel(r_ref, w_ref, *refs):
    index_refs, out_ref, values_ref = refs[:-2], refs[-2], refs[-1]
    values_ref[...] = lax.dot_general(
        quarters(r_ref[...]), w_ref[...], (((1,), (1,)), ((), ())), preferred_element_type=F32
    )
    for c, index_ref in enumerate(index_refs):
        gather_kept(values_ref, index_ref, out_ref, c * PER * PACKED, c * PACKED)


def latent_gradient(rows, weight, index):
    latents = weight.shape[0]
    total = GROUPS * CAP
    return pl.pallas_call(
        latent_gradient_kernel,
        out_shape=jax.ShapeDtypeStruct((total // PER, LANES), F32),
        in_specs=[whole()] * (2 + len(index)),
        out_specs=whole(),
        scratch_shapes=[pltpu.VMEM((total, latents), F32)],
        compiler_params=params(),
        cost_estimate=cost(4 * total * 1024 * latents, 4 << 20),
        name="latent_gradient",
    )(rows, weight, *index)


def spread_kept(kept_ref, low_ref, high_ref, dense_ref, tiles, source=0, target=0):
    for group in range(0, PACKED, 16):
        kept = kept_ref[source + group : source + group + 16, :]
        for q in range(PER):
            row = q * PACKED + group
            for column, t in enumerate(tiles):
                word_ref = (low_ref, high_ref)[t // 4]
                which = (word_ref[row : row + 16, :] >> (6 * (t % 4))) & 63
                spot = jnp.maximum(which - 1, 0) + q * KEPT
                taken = jnp.take_along_axis(kept, spot, axis=1, mode="promise_in_bounds")
                dense_ref[target + row : target + row + 16, column * LANES : (column + 1) * LANES] = (
                    jnp.where(which > 0, taken, 0.0).astype(BF16)
                )


def spread_latents(pre_ref, low_ref, high_ref, kept_ref, rows_ref):
    pre = pre_ref[...]
    kept_ref[...] = (pre / (1.0 + jnp.exp(-pre))).astype(BF16).astype(F32)
    tiles = range(rows_ref.shape[1] // LANES)
    spread_kept(kept_ref, low_ref, high_ref, rows_ref, tiles)


def decode_kernel(pre_ref, low_ref, high_ref, w_ref, out_ref, token_ref, kept_ref, rows_ref, made_ref, sem_ref):
    token_ref[...] = jnp.zeros_like(token_ref)
    spread_latents(pre_ref, low_ref, high_ref, kept_ref, rows_ref)
    copies = []
    inner = w_ref.shape[1]
    for j in range(inner // BLOCK):
        here = pl.ds(j * BLOCK, BLOCK)
        made_ref[:, here] = jnp.dot(
            rows_ref[...], w_ref[:, here], preferred_element_type=F32
        ).astype(BF16)
        for q in range(PER):
            source = made_ref.at[pl.ds(q * PACKED, PACKED), here]
            target = out_ref.at[:, pl.ds(q * inner + j * BLOCK, BLOCK)]
            copies.append(pltpu.make_async_copy(source, target, sem_ref.at[j, q]))
            copies[-1].start()
    for copy in copies:
        copy.wait()


def anywhere():
    return pl.BlockSpec(memory_space=pl.ANY)


def decode(pre, low, high, weight, after):
    total = low.shape[0]
    latents, inner = weight.shape
    return pl.pallas_call(
        skipping(decode_kernel, 4, len(after)),
        out_shape=(hbm((PACKED, PER * inner), BF16), TOKEN),
        in_specs=[whole()] * (4 + len(after)),
        out_specs=(anywhere(), whole()),
        scratch_shapes=[
            pltpu.VMEM(pre.shape, F32),
            pltpu.VMEM((total, latents), BF16),
            pltpu.VMEM((total, inner), BF16),
            pltpu.SemaphoreType.DMA((inner // BLOCK, PER)),
        ],
        compiler_params=params(),
        cost_estimate=cost(4 * total * inner * latents, 6 << 20),
        name="decode",
    )(pre, low, high, weight, *after)


def latents_kernel(*refs):
    count = len(CHUNKS)
    pre_refs, map_refs = refs[:count], refs[count : 3 * count]
    out_refs, token_ref, rows_refs = refs[3 * count : 4 * count], refs[4 * count], refs[4 * count + 1 : 5 * count + 1]
    kept_refs, sem_ref = refs[5 * count + 1 : -1], refs[-1]
    token_ref[...] = jnp.zeros_like(token_ref)
    copies = []
    for c in range(count):
        spread_latents(pre_refs[c], *map_refs[2 * c : 2 * c + 2], kept_refs[c], rows_refs[c])
        copies.append(pltpu.make_async_copy(rows_refs[c], out_refs[c], sem_ref.at[c]))
        copies[-1].start()
    for copy in copies:
        copy.wait()


def make_latents(pre, maps, latents):
    rows = [p.shape[0] * PER for p in pre]
    *out, token = pl.pallas_call(
        latents_kernel,
        out_shape=tuple(hbm((n, latents), BF16) for n in rows) + (TOKEN,),
        in_specs=[whole()] * (3 * len(pre)),
        out_specs=(anywhere(),) * len(pre) + (whole(),),
        scratch_shapes=[pltpu.VMEM((n, latents), BF16) for n in rows]
        + [pltpu.VMEM(p.shape, F32) for p in pre]
        + [pltpu.SemaphoreType.DMA((len(pre),))],
        compiler_params=params(),
        cost_estimate=cost(4_000_000_000, 4 << 20),
        name="make_latents",
    )(*pre, *[m for pair in maps for m in pair])
    return out, token


def residual_kernel(*refs):
    count = len(CHUNKS)
    info_ref, x_ref, bias_ref = refs[:3]
    back_refs, send_ref = refs[3 : 3 + count], refs[3 + count]
    tokens = x_ref.shape[0]
    info = info_ref[...]
    width = x_ref.shape[1]
    first = quarter_keys(tokens)
    keys = token_keys(info)
    hits = []
    for i in range(count * PER):
        slot = first + i * PLACES
        hits.append(as_ones((slot == keys[0]) | (slot == keys[1])))
    total = jnp.zeros(x_ref.shape, F32)
    for c, back_ref in enumerate(back_refs):
        total = total + lax.dot_general(
            jnp.concatenate(hits[c * PER : (c + 1) * PER], axis=0),
            quarters(back_ref[...]),
            (((0,), (0,)), ((), ())),
            preferred_element_type=F32,
        )
    residual = (total + bias_ref[...] - x_ref[...].astype(F32)).astype(BF16)
    for i, hit in enumerate(hits):
        send_ref[:, i * width : (i + 1) * width] = jnp.dot(
            hit, residual, preferred_element_type=F32
        ).astype(BF16)


def form_residual(info, x, bias, back, after):
    tokens, width = x.shape
    return pl.pallas_call(
        skipping(residual_kernel, 3 + len(CHUNKS), len(after)),
        out_shape=jax.ShapeDtypeStruct((PACKED, len(CHUNKS) * PER * width), BF16),
        in_specs=[whole()] * (3 + len(CHUNKS) + len(after)),
        out_specs=whole(),
        compiler_params=params(),
        cost_estimate=cost(4 * GROUPS * CAP * tokens * width, 5 << 20),
        name="form_residual",
    )(info, x, bias, *back, *after)


def turn_kernel(*refs):
    half = (len(refs) - 1) // 2
    refs[-1][...] = jnp.zeros(refs[-1].shape, F32)
    for src, dst in zip(refs[:half], refs[half:]):
        block = dst.shape[0]
        for q in range(PER):
            start = q * block * pl.num_programs(0) + pl.program_id(0) * block
            here = pl.ds(pl.multiple_of(start, block), block)
            dst[:, q * PACKED : (q + 1) * PACKED] = src[:, here].T


def turn(arrived, inner):
    return pl.pallas_call(
        turn_kernel,
        grid=(4,),
        out_shape=tuple(hbm((inner, PER * PACKED), BF16) for a in arrived) + (TOKEN,),
        in_specs=[whole()] * len(arrived),
        out_specs=tuple(pl.BlockSpec((inner // 4, PER * PACKED), lambda i: (i, 0)) for a in arrived)
        + (token_spec(),),
        compiler_params=params(),
        cost_estimate=cost(4_000_000_000, 4 << 20),
        name="turn_rows",
    )(*arrived)


def encoder_grad_kernel(scale, lg_ref, *refs):
    count = len(CHUNKS)
    pre_refs, map_refs, x_refs = refs[:count], refs[count : 3 * count], refs[3 * count : 4 * count]
    out_ref, kept_ref, grad_ref, made_ref = refs[4 * count : 4 * count + 4]
    held_refs, read_sem, sem_ref = refs[4 * count + 4 : -2], refs[-2], refs[-1]
    reads = [
        pltpu.make_async_copy(x_ref, held_ref, read_sem.at[c])
        for c, (x_ref, held_ref) in enumerate(zip(x_refs, held_refs))
    ]
    for copy in reads:
        copy.start()
    starts, start = [], 0
    for c, cap in enumerate(CHUNKS):
        packed = GROUPS * cap // PER
        pre = pre_refs[c][...]
        sig = 1.0 / (1.0 + jnp.exp(-pre))
        slope = lg_ref[start : start + packed, :] * (sig * (1.0 + pre * (1.0 - sig)))
        kept_ref[start : start + packed, :] = slope.astype(BF16).astype(F32)
        starts.append(start)
        start += packed

    def spread(j):
        for c, cap in enumerate(CHUNKS):
            tiles = range(j * BLOCK // LANES, (j + 1) * BLOCK // LANES)
            words = map_refs[2 * c : 2 * c + 2]
            spread_kept(kept_ref, *words, grad_ref.at[j], tiles, starts[c], starts[c] * PER)

    blocks = grad_ref.shape[0]
    spread(0)
    for copy in reads:
        copy.wait()
    writes = []
    for j in range(blocks):
        if j + 1 < blocks:
            spread(j + 1)
        total = None
        for c, cap in enumerate(CHUNKS):
            rows = slice(starts[c] * PER, starts[c] * PER + GROUPS * cap)
            part = jnp.dot(held_refs[c][...], grad_ref[j, rows, :], preferred_element_type=F32)
            total = part if total is None else total + part
        made_ref[j] = (total * scale).astype(BF16)
        copy = pltpu.make_async_copy(
            made_ref.at[j], out_ref.at[:, pl.ds(j * BLOCK, BLOCK)], sem_ref.at[j]
        )
        copy.start()
        writes.append(copy)
    for copy in writes:
        copy.wait()


def encoder_grad(lg, pre, maps, turned, scale):
    latents = 1024
    inner = turned[0].shape[0]
    blocks = latents // BLOCK
    operands = [lg, *pre, *[m for pair in maps for m in pair]]
    return pl.pallas_call(
        functools.partial(encoder_grad_kernel, scale),
        out_shape=jax.ShapeDtypeStruct((inner, latents), BF16),
        in_specs=[whole()] * len(operands) + [anywhere()] * len(turned),
        out_specs=anywhere(),
        scratch_shapes=[
            pltpu.VMEM(lg.shape, F32),
            pltpu.VMEM((blocks, GROUPS * CAP, BLOCK), BF16),
            pltpu.VMEM((blocks, inner, BLOCK), BF16),
        ]
        + [pltpu.VMEM(t.shape, BF16) for t in turned]
        + [pltpu.SemaphoreType.DMA((len(turned),)), pltpu.SemaphoreType.DMA((blocks,))],
        compiler_params=params(),
        cost_estimate=cost(4 * 1024 * inner * latents, 6 << 20),
        name="encoder_grad",
    )(*operands, *[in_hbm(t) for t in turned])


def decoder_grad_kernel(*refs):
    latent_refs, res_ref, out_ref, token_ref = refs[:-3], refs[-3], refs[-2], refs[-1]
    token_ref[...] = jnp.zeros_like(token_ref)
    block = out_ref.shape[0]
    here = pl.ds(pl.multiple_of(pl.program_id(0) * block, block), block)
    total = None
    width = out_ref.shape[1]
    for c, latent_ref in enumerate(latent_refs):
        part = lax.dot_general(
            latent_ref[:, here],
            quarters(res_ref[:, c * PER * width : (c + 1) * PER * width]),
            (((0,), (0,)), ((), ())),
            preferred_element_type=F32,
        )
        total = part if total is None else total + part
    out_ref[...] = total.astype(BF16)


def decoder_grad(latent, res):
    latents, inner = latent[0].shape[1], 1024
    block = 256
    return pl.pallas_call(
        decoder_grad_kernel,
        grid=(latents // block,),
        out_shape=(jax.ShapeDtypeStruct((latents, inner), BF16), TOKEN),
        in_specs=[whole()] * (len(latent) + 1),
        out_specs=(pl.BlockSpec((block, inner), lambda i: (i, 0)), token_spec()),
        compiler_params=params(),
        cost_estimate=cost(2 * 1024 * inner * latents, 6 << 20),
        name="decoder_grad",
    )(*latent, res)


def exchange(rows):
    count, width = rows.shape
    return lax.all_to_all(
        rows.reshape(GROUPS, count // GROUPS, width), "feat", split_axis=0, concat_axis=0, tiled=True
    ).reshape(count, width)


def add_kernel(*refs):
    total = refs[0][...]
    for ref in refs[1:-1]:
        total = total + ref[...]
    refs[-1][...] = total


def add_after(parts, after):
    return pl.pallas_call(
        skipping(add_kernel, len(parts), 1),
        out_shape=jax.ShapeDtypeStruct(parts[0].shape, F32),
        in_specs=[whole()] * (len(parts) + 1),
        out_specs=whole(),
        compiler_params=params(),
        name="add_parts",
    )(*parts, after)


def width_sum(part, between=None):
    for masks in ((1,), (4, 8, 12), (2,)):
        size = lax.axis_size("width")
        moved = [lax.ppermute(part, "width", [(a, a ^ m) for a in range(size)]) for m in masks]
        if between is not None and len(masks) > 1:
            part = add_after([part, *moved], between)
            continue
        for other in moved:
            part = part + other
    return part


def per_device(acts, enc_weight, enc_bias, dec_weight, dec_bias, routes, latent_index):
    tokens, layers, width_dev = acts.shape
    inner = layers * width_dev
    latents = enc_weight.shape[3]
    scale = 1.0 / math.sqrt(L * D)
    x_home = in_vmem(acts.reshape(tokens, inner))
    enc = enc_weight.reshape(inner, latents)
    dec = in_vmem(dec_weight.reshape(latents, inner))
    bias = jnp.where(lax.axis_index("width") == 0, enc_bias, 0.0)

    info, *sends = pack(routes.T, x_home, latent_index.reshape(tokens, 2 * KEPT))
    arrived = [exchange(s) for s in sends]
    index, maps = zip(*[slot_maps(a) for a in arrived])

    pre, back, after = [], [], ()
    for c in range(len(CHUNKS)):
        if c == 0:
            part = encode(arrived[c], in_vmem(enc), bias, index[c], after)
        else:
            part = encode_streamed(arrived[c], enc, bias, index[c], after)
        pre.append(width_sum(part))
        decoded, token = decode(pre[c], *maps[c], dec, ())
        after = (token,)
        back.append(exchange(decoded))

    *turned, token = turn(arrived, inner)
    latent, later = make_latents(pre, maps, latents)
    res = exchange(form_residual(info, x_home, dec_bias.reshape(1, inner), back, (token, later)))
    grad_dec, token = decoder_grad(latent, res)
    lg = width_sum(latent_gradient(res, dec, index), token)
    grad_enc = encoder_grad(lg, pre, maps, turned, scale)
    return (
        grad_enc.reshape(1, layers, width_dev, latents),
        grad_dec.reshape(1, latents, layers, width_dev),
    )


def solution(mesh):
    placed = (
        P("feat", None, "width"),
        P("feat", None, "width", None),
        P("feat", None),
        P("feat", None, None, "width"),
        P(None, "width"),
        P("feat", None),
        P("feat", None, None),
    )
    return jax.shard_map(
        per_device,
        mesh=mesh,
        in_specs=placed,
        out_specs=(P("feat", None, "width", None), P("feat", None, None, "width")),
        check_vma=False,
    )
```

```python
import functools
import math

import jax
import jax.numpy as jnp
from jax import lax
from jax.experimental import pallas as pl
from jax.experimental.pallas import tpu as pltpu
from jax.sharding import PartitionSpec as P

D = 8192
L = 2
CAP = 64
GROUPS = 16
CHUNKS = (32, 32)
LANES = 128
BLOCK = 256
KEPT = 32
PER = LANES // KEPT
BF16 = jnp.bfloat16
F32 = jnp.float32
I32 = jnp.int32
VMEM_LIMIT = 20 * 1024 * 1024


def iota(shape, dim):
    return lax.broadcasted_iota(I32, shape, dim)


def params():
    return pltpu.CompilerParams(vmem_limit_bytes=VMEM_LIMIT)


def cost(flops, nbytes):
    return pl.CostEstimate(flops=int(flops), bytes_accessed=int(nbytes), transcendentals=0)


def hbm(shape, dtype):
    return pltpu.HBM(shape, dtype)


def vmem(shape, dtype):
    return pltpu.VMEM(shape, dtype)


def in_hbm(x):
    return pltpu.with_memory_space_constraint(x, pltpu.HBM)


def in_vmem(x):
    return pltpu.with_memory_space_constraint(x, pltpu.VMEM)


def whole():
    return pl.BlockSpec(memory_space=pltpu.VMEM)


PLACES = CHUNKS[0] // PER
PACKED = GROUPS * PLACES


def quarter_keys(tokens):
    row = iota((PACKED, tokens), 0)
    return (row // PLACES) * CAP + row % PLACES


def token_keys(info):
    return [info[2 * j : 2 * j + 1] * CAP + info[2 * j + 1 : 2 * j + 2] for j in range(2)]


def as_ones(hit):
    return hit.astype(F32).astype(BF16)


def quarters(x, width=1024):
    return jnp.concatenate([x[:, i * width : (i + 1) * width] for i in range(x.shape[1] // width)], axis=0)


def pack_kernel(routes_ref, acts_ref, index_ref, info_ref, *send_refs):
    tokens, inner = acts_ref.shape
    upper = as_ones(iota((tokens, tokens), 0) < iota((tokens, tokens), 1))
    experts = iota((GROUPS, tokens), 0)
    total = jnp.zeros((GROUPS, 1), F32)
    rows = []
    for j in range(2):
        route = routes_ref[j : j + 1, :]
        hit = experts == route
        hot = hit.astype(F32)
        before = jnp.dot(hot.astype(BF16), upper, preferred_element_type=F32) + total
        total = total + jnp.sum(hot, axis=1, keepdims=True)
        pos = jnp.sum(jnp.where(hit, before, 0.0), axis=0, keepdims=True).astype(I32)
        rows += [route, pos]
    info = jnp.concatenate(rows + [jnp.zeros((4, tokens), I32)], axis=0)
    info_ref[...] = info
    x = acts_ref[...]
    index = index_ref[...]
    code = (((index & 127) + 128) << (index >> 7)).astype(F32).astype(BF16)
    cols = index.shape[1]
    col = iota((cols, LANES), 0)
    lane = iota((cols, LANES), 1)
    codes = [
        jnp.dot(code, as_ones(col == j * KEPT + lane % KEPT), preferred_element_type=F32).astype(BF16)
        for j in range(2)
    ]
    first = quarter_keys(tokens)
    keys = token_keys(info)
    lane_q = iota((PACKED, LANES), 1) // KEPT
    for c, send_ref in enumerate(send_refs):
        kept = jnp.zeros((PACKED, LANES), F32)
        for q in range(PER):
            slot = first + (c * PER + q) * PLACES
            hits = [slot == key for key in keys]
            send_ref[:, q * inner : (q + 1) * inner] = jnp.dot(
                as_ones(hits[0] | hits[1]), x, preferred_element_type=F32
            ).astype(BF16)
            for hit, route_codes in zip(hits, codes):
                picked = jnp.dot(as_ones(hit), route_codes, preferred_element_type=F32)
                kept = kept + jnp.where(lane_q == q, picked, 0.0)
        start = PER * inner + c * LANES
        send_refs[0][:, start : start + LANES] = kept.astype(BF16)


def pack(routes_t, x, index):
    tokens, width = x.shape
    widths = [PER * width + len(CHUNKS) * LANES] + [PER * width] * (len(CHUNKS) - 1)
    return pl.pallas_call(
        pack_kernel,
        out_shape=(jax.ShapeDtypeStruct((8, tokens), I32),)
        + tuple(jax.ShapeDtypeStruct((PACKED, w), BF16) for w in widths),
        in_specs=[whole()] * 3,
        out_specs=(whole(),) * (1 + len(CHUNKS)),
        compiler_params=params(),
        cost_estimate=cost(2 * GROUPS * CAP * tokens * width, 3 << 20),
        name="pack_tokens",
    )(routes_t, x, index)


def maps_kernel(codes_ref, index_ref, low_ref, high_ref, token_ref, scratch_ref):
    token_ref[...] = jnp.zeros_like(token_ref)
    code = codes_ref[...].astype(F32).astype(I32)
    tile = jnp.zeros(code.shape, I32)
    for h in range(7):
        tile = tile + jnp.where(code >= (256 << h), 1, 0)
    numbers = jnp.where(code > 0, tile * 128 + (code >> tile) - 128, -1)
    index_ref[...] = numbers
    turned = numbers.T
    tile = turned >> 7
    scratch_ref[0] = jnp.where(turned >= 0, turned & 127, -1)
    place = (iota(turned.shape, 0) % KEPT) + 1
    scratch_ref[1] = jnp.where((tile >= 0) & (tile < 4), place << (jnp.clip(tile, 0, 3) * 6), 0)
    scratch_ref[2] = jnp.where(tile >= 4, place << (jnp.clip(tile - 4, 0, 3) * 6), 0)
    for q in range(PER):
        lows, highs = [], []
        for part in range(2):
            size = LANES // 2
            spot = iota((size, LANES), 0) + part * size
            low = jnp.zeros((size, LANES), I32)
            high = jnp.zeros((size, LANES), I32)
            for k in range(KEPT):
                at = q * KEPT + k
                same = spot == scratch_ref[0, at : at + 1, :]
                low = low + jnp.where(same, scratch_ref[1, at : at + 1, :], 0)
                high = high + jnp.where(same, scratch_ref[2, at : at + 1, :], 0)
            lows.append(low)
            highs.append(high)
        rows = slice(q * PACKED, (q + 1) * PACKED)
        low_ref[rows, :] = jnp.concatenate(lows, axis=0).T
        high_ref[rows, :] = jnp.concatenate(highs, axis=0).T


def slot_maps(arrived, chunk):
    rows, width = arrived.shape
    block = width // LANES - len(CHUNKS) + chunk
    shapes = [jax.ShapeDtypeStruct((PACKED, LANES), I32)]
    shapes += [jax.ShapeDtypeStruct((PER * PACKED, LANES), I32)] * 2
    shapes.append(TOKEN)
    index, low, high, token = pl.pallas_call(
        maps_kernel,
        grid=(1,),
        out_shape=tuple(shapes),
        in_specs=[pl.BlockSpec((rows, LANES), lambda i: (0, block))],
        out_specs=tuple(pl.BlockSpec(s.shape, lambda i: (0, 0)) for s in shapes),
        scratch_shapes=[pltpu.VMEM((3, LANES, LANES), I32)],
        compiler_params=params(),
        cost_estimate=cost(2_000_000_000, 1 << 20),
        name="slot_maps",
    )(arrived)
    return index, (low, high), token


def skipping(kernel, inputs, extra):
    def run(*refs):
        kernel(*refs[:inputs], *refs[inputs + extra :])

    return run


TOKEN = jax.ShapeDtypeStruct((8, LANES), F32)


def token_spec():
    return pl.BlockSpec((8, LANES), lambda *i: (0, 0))


def gather_kept(values_ref, index_ref, out_ref, base, start):
    tiles = values_ref.shape[1] // LANES
    lane_q = iota((8, LANES), 1) // KEPT
    for group in range(0, PACKED, 8):
        idx = index_ref[group : group + 8, :]
        spot, tile = idx & 127, idx >> 7
        result = jnp.zeros((8, LANES), F32)
        for q in range(PER):
            row = base + q * PACKED + group
            here = jnp.where(lane_q == q, tile, -1)
            for t in range(tiles):
                part = values_ref[row : row + 8, t * LANES : (t + 1) * LANES]
                taken = jnp.take_along_axis(part, spot, axis=1, mode="promise_in_bounds")
                result = jnp.where(here == t, taken, result)
        out_ref[start + group : start + group + 8, :] = result


def encode_kernel(x_ref, w_ref, bias_ref, index_ref, out_ref, values_ref):
    x = quarters(x_ref[:, : PER * w_ref.shape[0]])
    values_ref[...] = jnp.dot(x, w_ref[...], preferred_element_type=F32) + bias_ref[...]
    gather_kept(values_ref, index_ref, out_ref, 0, 0)


def encode(rows, weight, bias, index, after):
    inner, latents = weight.shape
    return pl.pallas_call(
        skipping(encode_kernel, 4, len(after)),
        out_shape=jax.ShapeDtypeStruct((PACKED, LANES), F32),
        in_specs=[whole()] * (4 + len(after)),
        out_specs=whole(),
        scratch_shapes=[pltpu.VMEM((PER * PACKED, latents), F32)],
        compiler_params=params(),
        cost_estimate=cost(4 * PER * PACKED * inner * latents, 4 << 20),
        name="encode",
    )(rows, weight, bias, index, *after)


def encode_streamed_kernel(x_ref, w_ref, bias_ref, index_ref, out_ref, values_ref, x_held, w_held, sem_ref):
    inner, latents = w_ref.shape
    steps = inner // BLOCK
    reads = []
    for k in range(steps):
        here = pl.ds(k * BLOCK, BLOCK)
        reads.append([pltpu.make_async_copy(w_ref.at[here, :], w_held.at[here, :], sem_ref.at[PER, k])])
        for q in range(PER):
            source = x_ref.at[:, pl.ds(q * inner + k * BLOCK, BLOCK)]
            target = x_held.at[pl.ds(q * PACKED, PACKED), here]
            reads[-1].append(pltpu.make_async_copy(source, target, sem_ref.at[q, k]))
        for copy in reads[-1]:
            copy.start()
    for k in range(steps):
        for copy in reads[k]:
            copy.wait()
        here = pl.ds(k * BLOCK, BLOCK)
        part = jnp.dot(x_held[:, here], w_held[here, :], preferred_element_type=F32)
        if k == 0:
            values_ref[...] = part + bias_ref[...]
        else:
            values_ref[...] += part
    gather_kept(values_ref, index_ref, out_ref, 0, 0)


def encode_streamed(rows, weight, bias, index, after):
    total, (inner, latents) = PER * PACKED, weight.shape
    return pl.pallas_call(
        skipping(encode_streamed_kernel, 4, len(after)),
        out_shape=jax.ShapeDtypeStruct((PACKED, LANES), F32),
        in_specs=[pl.BlockSpec(memory_space=pl.ANY)] * 2 + [whole()] * (2 + len(after)),
        out_specs=whole(),
        scratch_shapes=[
            pltpu.VMEM((total, latents), F32),
            pltpu.VMEM((total, inner), BF16),
            pltpu.VMEM((inner, latents), BF16),
            pltpu.SemaphoreType.DMA((PER + 1, inner // BLOCK)),
        ],
        compiler_params=params(),
        cost_estimate=cost(4 * total * inner * latents, 4 << 20),
        name="encode_streamed",
    )(in_hbm(rows), in_hbm(weight), bias, index, *after)


def latent_gradient_kernel(r_ref, w_ref, *refs):
    index_refs, out_ref, values_ref = refs[:-2], refs[-2], refs[-1]
    values_ref[...] = lax.dot_general(
        quarters(r_ref[...]), w_ref[...], (((1,), (1,)), ((), ())), preferred_element_type=F32
    )
    for c, index_ref in enumerate(index_refs):
        gather_kept(values_ref, index_ref, out_ref, c * PER * PACKED, c * PACKED)


def latent_gradient(rows, weight, index):
    latents = weight.shape[0]
    total = GROUPS * CAP
    return pl.pallas_call(
        latent_gradient_kernel,
        out_shape=jax.ShapeDtypeStruct((total // PER, LANES), F32),
        in_specs=[whole()] * (2 + len(index)),
        out_specs=whole(),
        scratch_shapes=[pltpu.VMEM((total, latents), F32)],
        compiler_params=params(),
        cost_estimate=cost(4 * total * 1024 * latents, 4 << 20),
        name="latent_gradient",
    )(rows, weight, *index)


def spread_kept(kept_ref, low_ref, high_ref, dense_ref, tiles, source=0, target=0):
    for group in range(0, PACKED, 16):
        kept = kept_ref[source + group : source + group + 16, :]
        for q in range(PER):
            row = q * PACKED + group
            for column, t in enumerate(tiles):
                word_ref = (low_ref, high_ref)[t // 4]
                which = (word_ref[row : row + 16, :] >> (6 * (t % 4))) & 63
                spot = jnp.maximum(which - 1, 0) + q * KEPT
                taken = jnp.take_along_axis(kept, spot, axis=1, mode="promise_in_bounds")
                dense_ref[target + row : target + row + 16, column * LANES : (column + 1) * LANES] = (
                    jnp.where(which > 0, taken, 0.0).astype(BF16)
                )


def spread_latents(pre_ref, low_ref, high_ref, kept_ref, rows_ref):
    pre = pre_ref[...]
    kept_ref[...] = (pre / (1.0 + jnp.exp(-pre))).astype(BF16).astype(F32)
    tiles = range(rows_ref.shape[1] // LANES)
    spread_kept(kept_ref, low_ref, high_ref, rows_ref, tiles)


def decode_kernel(pre_ref, low_ref, high_ref, w_ref, out_ref, token_ref, kept_ref, rows_ref, made_ref, sem_ref):
    token_ref[...] = jnp.zeros_like(token_ref)
    spread_latents(pre_ref, low_ref, high_ref, kept_ref, rows_ref)
    copies = []
    inner = w_ref.shape[1]
    for j in range(inner // BLOCK):
        here = pl.ds(j * BLOCK, BLOCK)
        made_ref[:, here] = jnp.dot(
            rows_ref[...], w_ref[:, here], preferred_element_type=F32
        ).astype(BF16)
        for q in range(PER):
            source = made_ref.at[pl.ds(q * PACKED, PACKED), here]
            target = out_ref.at[:, pl.ds(q * inner + j * BLOCK, BLOCK)]
            copies.append(pltpu.make_async_copy(source, target, sem_ref.at[j, q]))
            copies[-1].start()
    for copy in copies:
        copy.wait()


def anywhere():
    return pl.BlockSpec(memory_space=pl.ANY)


def decode(pre, low, high, weight, after):
    total = low.shape[0]
    latents, inner = weight.shape
    return pl.pallas_call(
        skipping(decode_kernel, 4, len(after)),
        out_shape=(hbm((PACKED, PER * inner), BF16), TOKEN),
        in_specs=[whole()] * (4 + len(after)),
        out_specs=(anywhere(), whole()),
        scratch_shapes=[
            pltpu.VMEM(pre.shape, F32),
            pltpu.VMEM((total, latents), BF16),
            pltpu.VMEM((total, inner), BF16),
            pltpu.SemaphoreType.DMA((inner // BLOCK, PER)),
        ],
        compiler_params=params(),
        cost_estimate=cost(4 * total * inner * latents, 6 << 20),
        name="decode",
    )(pre, low, high, weight, *after)


def latents_kernel(*refs):
    count = len(CHUNKS)
    pre_refs, map_refs = refs[:count], refs[count : 3 * count]
    out_refs, token_ref, rows_refs = refs[3 * count : 4 * count], refs[4 * count], refs[4 * count + 1 : 5 * count + 1]
    kept_refs, sem_ref = refs[5 * count + 1 : -1], refs[-1]
    token_ref[...] = jnp.zeros_like(token_ref)
    copies = []
    for c in range(count):
        spread_latents(pre_refs[c], *map_refs[2 * c : 2 * c + 2], kept_refs[c], rows_refs[c])
        copies.append(pltpu.make_async_copy(rows_refs[c], out_refs[c], sem_ref.at[c]))
        copies[-1].start()
    for copy in copies:
        copy.wait()


def make_latents(pre, maps, latents):
    rows = [p.shape[0] * PER for p in pre]
    *out, token = pl.pallas_call(
        latents_kernel,
        out_shape=tuple(hbm((n, latents), BF16) for n in rows) + (TOKEN,),
        in_specs=[whole()] * (3 * len(pre)),
        out_specs=(anywhere(),) * len(pre) + (whole(),),
        scratch_shapes=[pltpu.VMEM((n, latents), BF16) for n in rows]
        + [pltpu.VMEM(p.shape, F32) for p in pre]
        + [pltpu.SemaphoreType.DMA((len(pre),))],
        compiler_params=params(),
        cost_estimate=cost(4_000_000_000, 4 << 20),
        name="make_latents",
    )(*pre, *[m for pair in maps for m in pair])
    return out, token


def residual_kernel(*refs):
    count = len(CHUNKS)
    info_ref, x_ref, bias_ref = refs[:3]
    back_refs, send_ref = refs[3 : 3 + count], refs[3 + count]
    tokens = x_ref.shape[0]
    info = info_ref[...]
    width = x_ref.shape[1]
    first = quarter_keys(tokens)
    keys = token_keys(info)
    hits = []
    for i in range(count * PER):
        slot = first + i * PLACES
        hits.append(as_ones((slot == keys[0]) | (slot == keys[1])))
    total = jnp.zeros(x_ref.shape, F32)
    for c, back_ref in enumerate(back_refs):
        total = total + lax.dot_general(
            jnp.concatenate(hits[c * PER : (c + 1) * PER], axis=0),
            quarters(back_ref[...]),
            (((0,), (0,)), ((), ())),
            preferred_element_type=F32,
        )
    residual = (total + bias_ref[...] - x_ref[...].astype(F32)).astype(BF16)
    for i, hit in enumerate(hits):
        send_ref[:, i * width : (i + 1) * width] = jnp.dot(
            hit, residual, preferred_element_type=F32
        ).astype(BF16)


def form_residual(info, x, bias, back, after):
    tokens, width = x.shape
    return pl.pallas_call(
        skipping(residual_kernel, 3 + len(CHUNKS), len(after)),
        out_shape=jax.ShapeDtypeStruct((PACKED, len(CHUNKS) * PER * width), BF16),
        in_specs=[whole()] * (3 + len(CHUNKS) + len(after)),
        out_specs=whole(),
        compiler_params=params(),
        cost_estimate=cost(4 * GROUPS * CAP * tokens * width, 5 << 20),
        name="form_residual",
    )(info, x, bias, *back, *after)


def turn_kernel(*refs):
    half = (len(refs) - 1) // 2
    refs[-1][...] = jnp.zeros(refs[-1].shape, F32)
    for src, dst in zip(refs[:half], refs[half:]):
        block = dst.shape[0]
        for q in range(PER):
            start = q * block * pl.num_programs(0) + pl.program_id(0) * block
            here = pl.ds(pl.multiple_of(start, block), block)
            dst[:, q * PACKED : (q + 1) * PACKED] = src[:, here].T


def turn(arrived, inner):
    return pl.pallas_call(
        turn_kernel,
        grid=(4,),
        out_shape=tuple(hbm((inner, PER * PACKED), BF16) for a in arrived) + (TOKEN,),
        in_specs=[whole()] * len(arrived),
        out_specs=tuple(pl.BlockSpec((inner // 4, PER * PACKED), lambda i: (i, 0)) for a in arrived)
        + (token_spec(),),
        compiler_params=params(),
        cost_estimate=cost(4_000_000_000, 4 << 20),
        name="turn_rows",
    )(*arrived)


def encoder_grad_kernel(scale, lg_ref, *refs):
    count = len(CHUNKS)
    pre_refs, map_refs, x_refs = refs[:count], refs[count : 3 * count], refs[3 * count : 4 * count]
    out_ref, kept_ref, grad_ref, made_ref = refs[4 * count : 4 * count + 4]
    held_refs, read_sem, sem_ref = refs[4 * count + 4 : -2], refs[-2], refs[-1]
    reads = [
        pltpu.make_async_copy(x_ref, held_ref, read_sem.at[c])
        for c, (x_ref, held_ref) in enumerate(zip(x_refs, held_refs))
    ]
    for copy in reads:
        copy.start()
    starts, start = [], 0
    for c, cap in enumerate(CHUNKS):
        packed = GROUPS * cap // PER
        pre = pre_refs[c][...]
        sig = 1.0 / (1.0 + jnp.exp(-pre))
        slope = lg_ref[start : start + packed, :] * (sig * (1.0 + pre * (1.0 - sig)))
        kept_ref[start : start + packed, :] = slope.astype(BF16).astype(F32)
        starts.append(start)
        start += packed

    def spread(j):
        for c, cap in enumerate(CHUNKS):
            tiles = range(j * BLOCK // LANES, (j + 1) * BLOCK // LANES)
            words = map_refs[2 * c : 2 * c + 2]
            spread_kept(kept_ref, *words, grad_ref.at[j], tiles, starts[c], starts[c] * PER)

    blocks = grad_ref.shape[0]
    spread(0)
    for copy in reads:
        copy.wait()
    writes = []
    for j in range(blocks):
        if j + 1 < blocks:
            spread(j + 1)
        total = None
        for c, cap in enumerate(CHUNKS):
            rows = slice(starts[c] * PER, starts[c] * PER + GROUPS * cap)
            part = jnp.dot(held_refs[c][...], grad_ref[j, rows, :], preferred_element_type=F32)
            total = part if total is None else total + part
        made_ref[j] = (total * scale).astype(BF16)
        copy = pltpu.make_async_copy(
            made_ref.at[j], out_ref.at[:, pl.ds(j * BLOCK, BLOCK)], sem_ref.at[j]
        )
        copy.start()
        writes.append(copy)
    for copy in writes:
        copy.wait()


def encoder_grad(lg, pre, maps, turned, scale):
    latents = 1024
    inner = turned[0].shape[0]
    blocks = latents // BLOCK
    operands = [lg, *pre, *[m for pair in maps for m in pair]]
    return pl.pallas_call(
        functools.partial(encoder_grad_kernel, scale),
        out_shape=jax.ShapeDtypeStruct((inner, latents), BF16),
        in_specs=[whole()] * len(operands) + [anywhere()] * len(turned),
        out_specs=anywhere(),
        scratch_shapes=[
            pltpu.VMEM(lg.shape, F32),
            pltpu.VMEM((blocks, GROUPS * CAP, BLOCK), BF16),
            pltpu.VMEM((blocks, inner, BLOCK), BF16),
        ]
        + [pltpu.VMEM(t.shape, BF16) for t in turned]
        + [pltpu.SemaphoreType.DMA((len(turned),)), pltpu.SemaphoreType.DMA((blocks,))],
        compiler_params=params(),
        cost_estimate=cost(4 * 1024 * inner * latents, 6 << 20),
        name="encoder_grad",
    )(*operands, *[in_hbm(t) for t in turned])


def decoder_grad_kernel(*refs):
    latent_refs, res_ref, out_ref, token_ref = refs[:-3], refs[-3], refs[-2], refs[-1]
    token_ref[...] = jnp.zeros_like(token_ref)
    block = out_ref.shape[0]
    here = pl.ds(pl.multiple_of(pl.program_id(0) * block, block), block)
    total = None
    width = out_ref.shape[1]
    for c, latent_ref in enumerate(latent_refs):
        part = lax.dot_general(
            latent_ref[:, here],
            quarters(res_ref[:, c * PER * width : (c + 1) * PER * width]),
            (((0,), (0,)), ((), ())),
            preferred_element_type=F32,
        )
        total = part if total is None else total + part
    out_ref[...] = total.astype(BF16)


def decoder_grad(latent, res):
    latents, inner = latent[0].shape[1], 1024
    block = 256
    return pl.pallas_call(
        decoder_grad_kernel,
        grid=(latents // block,),
        out_shape=(jax.ShapeDtypeStruct((latents, inner), BF16), TOKEN),
        in_specs=[whole()] * (len(latent) + 1),
        out_specs=(pl.BlockSpec((block, inner), lambda i: (i, 0)), token_spec()),
        compiler_params=params(),
        cost_estimate=cost(2 * 1024 * inner * latents, 6 << 20),
        name="decoder_grad",
    )(*latent, res)


def exchange(rows):
    count, width = rows.shape
    return lax.all_to_all(
        rows.reshape(GROUPS, count // GROUPS, width), "feat", split_axis=0, concat_axis=0, tiled=True
    ).reshape(count, width)


def add_kernel(*refs):
    total = refs[0][...]
    for ref in refs[1:-1]:
        total = total + ref[...]
    refs[-1][...] = total


def add_after(parts, after):
    return pl.pallas_call(
        skipping(add_kernel, len(parts), 1),
        out_shape=jax.ShapeDtypeStruct(parts[0].shape, F32),
        in_specs=[whole()] * (len(parts) + 1),
        out_specs=whole(),
        compiler_params=params(),
        name="add_parts",
    )(*parts, after)


def width_sum(part, between=None):
    for masks in ((1,), (4, 8, 12), (2,)):
        size = lax.axis_size("width")
        moved = [lax.ppermute(part, "width", [(a, a ^ m) for a in range(size)]) for m in masks]
        if between is not None and len(masks) > 1:
            part = add_after([part, *moved], between)
            continue
        for other in moved:
            part = part + other
    return part


def per_device(acts, enc_weight, enc_bias, dec_weight, dec_bias, routes, latent_index):
    tokens, layers, width_dev = acts.shape
    inner = layers * width_dev
    latents = enc_weight.shape[3]
    scale = 1.0 / math.sqrt(L * D)
    x_home = in_vmem(acts.reshape(tokens, inner))
    enc = enc_weight.reshape(inner, latents)
    dec = in_vmem(dec_weight.reshape(latents, inner))
    bias = jnp.where(lax.axis_index("width") == 0, enc_bias, 0.0)

    info, *sends = pack(routes.T, x_home, latent_index.reshape(tokens, 2 * KEPT))
    arrived = [exchange(s) for s in sends]
    index, maps, ready = zip(*[slot_maps(arrived[0], c) for c in range(len(CHUNKS))])

    pre, back, after = [], [], ()
    for c in range(len(CHUNKS)):
        if c == 0:
            part = encode(arrived[c], in_vmem(enc), bias, index[c], after)
        else:
            part = encode_streamed(arrived[c], enc, bias, index[c], after)
        pre.append(width_sum(part))
        decoded, token = decode(pre[c], *maps[c], dec, ready[1:] if c == 0 else ())
        after = (token,)
        back.append(exchange(decoded))

    *turned, token = turn(arrived, inner)
    latent, later = make_latents(pre, maps, latents)
    res = exchange(form_residual(info, x_home, dec_bias.reshape(1, inner), back, (token, later)))
    grad_dec, token = decoder_grad(latent, res)
    lg = width_sum(latent_gradient(res, dec, index), token)
    grad_enc = encoder_grad(lg, pre, maps, turned, scale)
    return (
        grad_enc.reshape(1, layers, width_dev, latents),
        grad_dec.reshape(1, latents, layers, width_dev),
    )


def solution(mesh):
    placed = (
        P("feat", None, "width"),
        P("feat", None, "width", None),
        P("feat", None),
        P("feat", None, None, "width"),
        P(None, "width"),
        P("feat", None),
        P("feat", None, None),
    )
    return jax.shard_map(
        per_device,
        mesh=mesh,
        in_specs=placed,
        out_specs=(P("feat", None, "width", None), P("feat", None, None, "width")),
        check_vma=False,
    )
```
